256 devices in a mesh: grp: 4 (over y), ep: 64 (over x, z, core).
Axes of the slice: x: 4, y: 4, z: 8, core: 2. Of those that a mesh axis runs over, the one named last changes fastest.
Arguments:
- tokens: bfloat16 [8192, 2048], P(('grp', 'ep')), may hold values from -6 to 6
- grad_out: bfloat16 [8192, 2048], P(('grp', 'ep')), may hold values from -0.29882812 to 0.29882812
- combine: bfloat16 [8192, 10], P(('grp', 'ep')), may hold values from 0.19921875 to 1.5
- expert_ids: int32 [8192, 10], P(('grp', 'ep')), may hold values from 0 to 63, all different within a row; in each aligned block of 32 rows (0 to 31, 32 to 63, ...) at most 16 rows name the same one
- w_gate: bfloat16 [64, 2048, 512], P('ep'), may hold values from -0.125 to 0.125
- w_up: bfloat16 [64, 2048, 512], P('ep'), may hold values from -0.125 to 0.125
- w_down: bfloat16 [64, 512, 2048], P('ep'), may hold values from -0.25 to 0.25
Outputs:
- grad_tokens: bfloat16 [8192, 2048], P(('grp', 'ep'))
- grad_combine: bfloat16 [8192, 10], P(('grp', 'ep'))
- grad_gate: bfloat16 [64, 2048, 512], P('ep', 'grp')
- grad_up: bfloat16 [64, 2048, 512], P('ep', 'grp')
- grad_down: bfloat16 [64, 512, 2048], P('ep', None, 'grp')
The draws below stay inside these ranges and needn't reach their ends.
Inputs may be any that keep to these rules, and one draw needn't show every extreme that they name: `expert_ids`: each row names 10 different experts. Within the rows of one device (aligned blocks of 32 rows) no expert is named by more than 16 rows, and in some block one expert is named by exactly 16 rows.
All inputs are finite; a program needn't handle non-finite values.
Results may differ from the reference program's by a relative error of at most 0.013.
Values may be sent and summed in bfloat16 or wider, within the bound.
A program may use at most 128 MiB of HBM per device.

```python
import math
import jax
import jax.numpy as jnp
import numpy as np
from jax import lax

D = 2048
FF = 512
TOK_DEV = 32
CAP = 16
EXPERTS = 64
TOPK = 10
TOKENS = 8192
N_GRP = 4
N_EP = 64


def steps_of(stream_key, dims, split, least, high):
    gain = 1.0
    for dim, parts in split:
        draws = jax.random.uniform(jax.random.fold_in(jax.random.fold_in(stream_key, 6), dim), (parts,), jnp.float32, least / len(split), high / len(split))
        gain = gain * jnp.repeat(jnp.exp(draws), dims[dim] // parts).reshape((-1,) + (1,) * (len(dims) - 1 - dim))
    return gain


def deal_out(key, own, number, rows, number_of, top, most, slope):
    sequence = jax.random.permutation(key, number_of)
    crowded, usual = load_shares(number_of, rows * top, most, slope, True), load_shares(number_of, rows * top, most, slope, False)
    places = jnp.arange(number_of)

    def named(tallies, turn):
        used = int((tallies > 0).sum())
        fixed = max(1, used // 4)
        passed = fixed + (places - fixed + turn * (used - fixed)) % max(1, number_of - fixed)
        return jnp.zeros((number_of,), jnp.int32).at[sequence[jnp.where(places < fixed, places, passed)]].set(jnp.asarray(tallies, jnp.int32))

    tallies = jnp.where(number % 4 == 0, named(crowded, number // 4), named(usual, number - number // 4 - 1))
    mixed = jax.random.permutation(jax.random.fold_in(own, 3), number_of)
    giver, sink = mixed[0:number_of // 2 * 2:2], mixed[1:number_of // 2 * 2:2]
    slack = jnp.minimum(tallies[giver] - 1, most - tallies[sink]) // 2
    slack = jnp.where((giver == sequence[0]) | (sink == sequence[0]) | (tallies[sink] == 0), 0, jnp.maximum(slack, 0))
    passed = jax.random.randint(jax.random.fold_in(own, 4), (number_of // 2,), 0, 1 << 20) % (slack + 1)
    tallies = tallies.at[giver].add(-passed).at[sink].add(passed)
    items = jnp.searchsorted(jnp.cumsum(tallies), jnp.arange(rows * top), side="right").astype(jnp.int32)
    grid = items.reshape(top, rows).T
    grid = grid[jax.random.permutation(jax.random.fold_in(own, 1), rows)]
    turn = jax.random.randint(jax.random.fold_in(own, 2), (rows, 1), 0, top)
    return jnp.take_along_axis(grid, (jnp.arange(top)[None, :] + turn) % top, axis=1)


def load_shares(amount, total, bound, lean, full):
    loads = [(1 << 20) // math.isqrt(grade ** lean) + 1 for grade in range(1, amount + 1)]
    largest = bound if full else min(bound, max(-(-total // amount), total * loads[0] // sum(loads)))
    least = 1 if total - largest >= amount - 1 else 0
    given, surplus = [largest] + [least] * (amount - 1), total - largest - least * (amount - 1)
    while surplus > 0:
        free = [i for i in range(1, amount) if given[i] < largest] or [i for i in range(1, amount) if given[i] < bound]
        pool, left = sum([loads[i] for i in free]), surplus
        for i in free:
            more = min(bound - given[i], max(1, left * loads[i] // pool), surplus)
            given[i] = given[i] + more
            surplus = surplus - more
    return np.array(given)


def bell_draw(rng, shape, deviation, bound, split=(), kind=jnp.bfloat16):
    entries = deviation * jax.random.normal(rng, shape, jnp.float32)
    if split:
        entries = entries * steps_of(rng, shape, split, -0.22, 0.18)
    return jnp.clip(entries, -bound, bound).astype(kind)


def setup_inputs(seed: int = 0) -> dict:
    key_list = jax.random.split(jax.random.key(seed), 8)
    tokens = bell_draw(key_list[0], (TOKENS, D), 1.0, 6.0, ((0, 256),))
    grad_out = bell_draw(key_list[1], (TOKENS, D), 0.05, 0.29882812, ((0, 256),))
    combine = jnp.clip(0.19921875 + 1.3007812 * jax.random.uniform(key_list[2], (TOKENS, TOPK), jnp.float32) ** steps_of(key_list[2], (TOKENS, TOPK), ((0, 256),), -0.2, 0.2), 0.19921875, 1.5).astype(jnp.bfloat16)
    expert_ids_keys = jax.random.split(jax.random.fold_in(key_list[3], 1), TOKENS // TOK_DEV)
    expert_ids_turns = jax.random.permutation(jax.random.fold_in(key_list[3], 3), TOKENS // TOK_DEV)
    expert_ids = jax.vmap(lambda own, number: deal_out(jax.random.fold_in(key_list[3], 2), own, number, TOK_DEV, EXPERTS, TOPK, CAP, 2))(expert_ids_keys, expert_ids_turns).reshape((TOKENS, TOPK))
    w_gate = bell_draw(key_list[4], (EXPERTS, D, FF), D ** -0.5, 0.125, ((0, 64),))
    w_up = bell_draw(key_list[5], (EXPERTS, D, FF), D ** -0.5, 0.125, ((0, 64),))
    w_down = bell_draw(key_list[6], (EXPERTS, FF, D), FF ** -0.5, 0.25, ((0, 64),))
    return {"tokens": tokens, "grad_out": grad_out, "combine": combine, "expert_ids": expert_ids, "w_gate": w_gate, "w_up": w_up, "w_down": w_down}


def dot_plain(left, right):
    return jnp.dot(left, right, preferred_element_type=jnp.float32)


def dot_back(left, right):
    return lax.dot_general(left, right, (((1,), (1,)), ((), ())), preferred_element_type=jnp.float32)


def dot_rows(left, right):
    return lax.dot_general(left, right, (((0,), (0,)), ((), ())), preferred_element_type=jnp.float32)


def expert_rows(rows_x, rows_dy, rows_w, gate_weight, up_weight, down_weight):
    pre_gate = dot_plain(rows_x, gate_weight)
    pre_up = dot_plain(rows_x, up_weight)
    sigmoid_gate = jax.nn.sigmoid(pre_gate)
    activation = pre_gate * sigmoid_gate
    derivative = sigmoid_gate * (1.0 + pre_gate * (1.0 - sigmoid_gate))
    hidden = (activation * pre_up).astype(jnp.bfloat16)
    output = dot_plain(hidden, down_weight)
    weight_grad = jnp.sum(rows_dy.astype(jnp.float32) * output, axis=1)
    scaled = (rows_w.astype(jnp.float32)[:, None] * rows_dy.astype(jnp.float32)).astype(jnp.bfloat16)
    grad_hidden = dot_back(scaled, down_weight)
    up_rows = (grad_hidden * activation).astype(jnp.bfloat16)
    gate_rows = (grad_hidden * pre_up * derivative).astype(jnp.bfloat16)
    grad_rows = (dot_back(gate_rows, gate_weight) + dot_back(up_rows, up_weight)).astype(jnp.bfloat16)
    return hidden, scaled, gate_rows, up_rows, grad_rows, weight_grad


def reference(tokens, grad_out, combine, expert_ids, w_gate, w_up, w_down):
    group_rows = TOK_DEV * N_EP * TOPK
    slot_count = N_EP * CAP
    flat_ids = expert_ids.reshape(-1).astype(jnp.int32)
    flat_w = combine.reshape(-1)

    def per_expert(carried, inputs):
        token_acc, combine_acc = carried
        expert, gate_weight, up_weight, down_weight = inputs
        totals = [jnp.zeros(gate_weight.shape, jnp.float32), jnp.zeros(up_weight.shape, jnp.float32),
                  jnp.zeros(down_weight.shape, jnp.float32)]
        for group_index in range(N_GRP):
            group_base = group_index * group_rows
            group_ids = flat_ids[group_base:group_base + group_rows]
            ordering = jnp.argsort((group_ids != expert).astype(jnp.int32), stable=True)[:slot_count].astype(jnp.int32)
            live_mask = group_ids[ordering] == expert
            entries_at = ordering + group_base
            token_of = entries_at // TOPK
            rows_x = jnp.where(live_mask[:, None], tokens[token_of], jnp.zeros((), jnp.bfloat16))
            rows_dy = jnp.where(live_mask[:, None], grad_out[token_of], jnp.zeros((), jnp.bfloat16))
            rows_w = jnp.where(live_mask, flat_w[entries_at], jnp.zeros((), jnp.bfloat16))
            hidden, scaled, gate_rows, up_rows, grad_rows, weight_grad = expert_rows(
                rows_x, rows_dy, rows_w, gate_weight, up_weight, down_weight)
            token_acc = token_acc.at[token_of].add(
                jnp.where(live_mask[:, None], grad_rows.astype(jnp.float32), jnp.zeros((), jnp.float32)))
            combine_acc = combine_acc.at[entries_at].add(
                jnp.where(live_mask, weight_grad, jnp.zeros((), jnp.float32)))
            partial_terms = (dot_rows(rows_x, gate_rows), dot_rows(rows_x, up_rows), dot_rows(hidden, scaled))
            for place in range(3):
                rounded = lax.optimization_barrier(partial_terms[place].astype(jnp.bfloat16))
                totals[place] = totals[place] + rounded.astype(jnp.float32)
        outputs = (totals[0].astype(jnp.bfloat16), totals[1].astype(jnp.bfloat16), totals[2].astype(jnp.bfloat16))
        return (token_acc, combine_acc), outputs

    start_state = (jnp.zeros((TOKENS, D), jnp.float32), jnp.zeros((TOKENS * TOPK,), jnp.float32))
    (token_acc, combine_acc), stacked = lax.scan(
        per_expert, start_state, (jnp.arange(EXPERTS, dtype=jnp.int32), w_gate, w_up, w_down))
    grad_tokens = token_acc.astype(jnp.bfloat16)
    grad_combine = combine_acc.reshape(TOKENS, TOPK).astype(jnp.bfloat16)
    return grad_tokens, grad_combine, stacked[0], stacked[1], stacked[2]
```

```python
import functools

import jax
import jax.numpy as jnp
from jax import lax
from jax.experimental import pallas as pl
from jax.experimental.pallas import tpu as pltpu
from jax.sharding import PartitionSpec as P

MESH = pl.DeviceIdType.MESH
F32 = jnp.float32
BF16 = jnp.bfloat16

NX, NZ, NG = 4, 8, 4
TOK = 32
HALF = TOK // 2
CAP = 16
LANES = 128
XO = (0, 1, -1, 2)
ZO = (0, 1, -1, 2, -2, 3, -3, 4)
BLOCKS = NX * NZ
CHUNK = 8
CTOK = CHUNK * TOK
CROW = CHUNK * CAP
ROUNDS = 2 * BLOCKS // CHUNK


def slot_of(kind, ox, oz):
    xi, zi = XO.index(ox), ZO.index(oz)
    return zi * NX + xi if kind == 0 else xi * NZ + zi


def dot(left, right, dims=((1,), (0,))):
    return lax.dot_general(left, right, (dims, ((), ())), preferred_element_type=F32)


def kernel(
    tokens,
    grad_out,
    combine,
    expert_ids,
    w_gate,
    w_up,
    w_down,
    o_tokens,
    o_combine,
    o_gate,
    o_up,
    o_down,
    buf,
    wg,
    wu,
    wd,
    rows_all,
    rows_t,
    pair,
    grads,
    sib,
    ysend,
    yrecv,
    xfar,
    xnear,
    znear,
    in_sem,
    ag_send,
    ag_recv,
    core_send,
    sib_send,
    sib_recv,
    y_send,
    y_recv,
    xf_send,
    xf_recv,
    xn_send,
    xn_recv,
    z_send,
    z_recv,
):
    width = tokens.shape[1]
    hidden_width = w_gate.shape[1]
    part = width // NG
    fhalf = hidden_width // 2
    grad_width = width + LANES
    me = lax.axis_index("ep")
    group = lax.axis_index("grp")
    core = me % 2
    zpos = (me // 2) % NZ
    xpos = me // (2 * NZ)

    def at(dx, dz):
        return {"ep": (((xpos + dx + NX) % NX) * NZ + (zpos + dz + NZ) % NZ) * 2 + core}

    sibling = {"ep": me + 1 - 2 * core}
    y_next = {"grp": (group + 1) % NG}
    y_prev = {"grp": (group + NG - 1) % NG}
    x_next, x_prev, z_next, z_prev = at(1, 0), at(-1, 0), at(0, 1), at(0, -1)

    barrier = pltpu.get_barrier_semaphore()
    for other in (sibling, x_next, x_prev, z_next, z_prev, y_next, y_prev):
        pl.semaphore_signal(barrier, inc=1, device_id=other, device_id_type=MESH)

    loads = [
        pltpu.make_async_copy(tokens, buf.at[core, pl.ds(0, TOK), pl.ds(0, width)], in_sem.at[0]),
        pltpu.make_async_copy(
            grad_out, buf.at[core, pl.ds(0, TOK), pl.ds(width, width)], in_sem.at[1]
        ),
        pltpu.make_async_copy(w_gate, wg, in_sem.at[2]),
        pltpu.make_async_copy(w_up, wu, in_sem.at[3]),
        pltpu.make_async_copy(w_down, wd, in_sem.at[4]),
    ]
    for load in loads:
        load.start()
    lane_iota = lax.broadcasted_iota(jnp.int32, (TOK, LANES), 1)
    ids = expert_ids[...]
    weights = combine[...].astype(F32)
    table = jnp.zeros((TOK, LANES), F32)
    for k in range(ids.shape[1]):
        table = table + jnp.where(ids[:, k : k + 1] == lane_iota, weights[:, k : k + 1], 0.0)
    buf[core, 0:TOK, 2 * width : 2 * width + LANES] = table.astype(BF16)
    loads[0].wait()
    loads[1].wait()
    pl.semaphore_wait(barrier, 7)

    hops, shares = ({}, {}), ({}, {})

    def span(slot, half):
        if half is None:
            return pl.ds(slot * TOK, TOK)
        return pl.ds(slot * TOK + half * HALF, HALF)

    def hop(kind, source, target, other, half=None):
        a, b = slot_of(kind, *source), slot_of(kind, *target)
        index = (kind * BLOCKS + b) * 2 + (half or 0)
        return pltpu.make_async_remote_copy(
            src_ref=buf.at[kind, span(a, half)],
            dst_ref=buf.at[kind, span(b, half)],
            send_sem=ag_send.at[index],
            recv_sem=ag_recv.at[index],
            device_id=other,
            device_id_type=MESH,
        )

    def send(kind, source, target, other, half=None):
        hop(kind, source, target, other, half).start()
        hops[kind][target, half] = source, other

    def across(kind, slot):
        return pltpu.make_async_remote_copy(
            src_ref=buf.at[kind, span(slot, None)],
            dst_ref=buf.at[kind, span(slot, None)],
            send_sem=core_send.at[slot],
            recv_sem=ag_recv.at[(kind * BLOCKS + slot) * 2],
            device_id=sibling,
            device_id_type=MESH,
        )

    def share(kind, offset):
        across(kind, slot_of(kind, *offset)).start()
        shares[kind][offset] = True

    def arrive(kind, offset, half=None):
        hop(kind, offset, offset, z_next, half).wait_recv()

    def z_out(kind, ox, oz):
        if oz == 0:
            send(kind, (ox, 0), (ox, 1), z_next)
            send(kind, (ox, 0), (ox, -1), z_prev)
        elif oz == 3:
            send(kind, (ox, 3), (ox, 4), z_next, half=0)
        elif oz == -3:
            send(kind, (ox, -3), (ox, 4), z_prev, half=1)
        elif oz > 0:
            send(kind, (ox, oz), (ox, oz + 1), z_next)
        else:
            send(kind, (ox, oz), (ox, oz - 1), z_prev)

    def x_out(oz):
        send(1, (0, oz), (1, oz), x_next)
        send(1, (0, oz), (-1, oz), x_prev)

    def first_round(kind):
        if kind == 0:
            send(0, (0, 0), (1, 0), x_next)
            send(0, (0, 0), (-1, 0), x_prev)
            z_out(0, 0, 0)
            share(0, (0, 0))
            arrive(0, (1, 0))
            send(0, (1, 0), (2, 0), x_next, half=0)
            z_out(0, 1, 0)
            share(0, (1, 0))
            arrive(0, (-1, 0))
            send(0, (-1, 0), (2, 0), x_prev, half=1)
            z_out(0, -1, 0)
            share(0, (-1, 0))
            arrive(0, (2, 0), 0)
            arrive(0, (2, 0), 1)
            z_out(0, 2, 0)
            share(0, (2, 0))
            z_round(1)
        else:
            z_out(1, 0, 0)
            x_out(0)
            share(1, (0, 0))
            for oz in (1, -1, 2, -2):
                arrive(1, (0, oz))
                z_out(1, 0, oz)
                x_out(oz)
                share(1, (0, oz))

    def z_round(k):
        for ox in XO:
            for oz in (k, -k):
                arrive(0, (ox, oz))
                z_out(0, ox, oz)
                share(0, (ox, oz))

    def z_last():
        for ox in XO:
            arrive(0, (ox, 4), 0)
            arrive(0, (ox, 4), 1)
            share(0, (ox, 4))

    def x_near(offsets):
        for oz in offsets:
            even = ZO.index(oz) % 2 == 0
            arrive(1, (1, oz))
            if even:
                send(1, (1, oz), (2, oz), x_next)
            share(1, (1, oz))
            arrive(1, (-1, oz))
            if not even:
                send(1, (-1, oz), (2, oz), x_prev)
            share(1, (-1, oz))

    def x_far(offsets):
        for oz in offsets:
            arrive(1, (2, oz))
            share(1, (2, oz))

    def second_round():
        for oz in (3, -3):
            arrive(1, (0, oz))
            z_out(1, 0, oz)
            x_out(oz)
            share(1, (0, oz))
        x_near((0,))
        arrive(1, (0, 4), 0)
        arrive(1, (0, 4), 1)
        x_out(4)
        share(1, (0, 4))

    plans = (
        {
            0: lambda: first_round(0),
            2: lambda: z_round(2),
            4: lambda: z_round(3),
            6: z_last,
        },
        {
            0: lambda: first_round(1),
            1: second_round,
            2: lambda: x_near((1, -1, 2, -2)),
            3: lambda: x_near((3, -3, 4)),
            5: lambda: x_far((0, 1, -1)),
            6: lambda: x_far((2, -2)),
            7: lambda: x_far((3, -3, 4)),
        },
    )

    def pair_copy(kind, rows):
        return pltpu.make_async_remote_copy(
            src_ref=grads.at[kind, rows],
            dst_ref=sib.at[rows],
            send_sem=sib_send.at[rows.start // CTOK],
            recv_sem=sib_recv.at[rows.start // CTOK],
            device_id=sibling,
            device_id_type=MESH,
        )

    def chunk(step, kind):
        first = pl.multiple_of((step // 2) * CTOK, CTOK)
        rows = pl.ds(first, CTOK)
        packed = pl.ds(pl.multiple_of(step * CROW, CROW), CROW)
        pick = (lax.broadcasted_iota(jnp.int32, (CAP, LANES), 1) == me).astype(F32).astype(BF16)
        table = buf[kind, rows, 2 * width : 2 * width + LANES]
        weight_row = dot(pick, table, ((1,), (1,)))
        routed = jnp.where(weight_row > 0, 1.0, 0.0)
        row_id = lax.broadcasted_iota(jnp.int32, (CTOK, CTOK), 0)
        col_id = lax.broadcasted_iota(jnp.int32, (CTOK, CTOK), 1)
        upto = (row_id <= col_id) & (row_id // TOK == col_id // TOK)
        rank = dot(routed.astype(BF16), upto.astype(F32).astype(BF16))
        base = (lax.broadcasted_iota(jnp.int32, (1, CTOK), 1) // TOK * CAP).astype(F32)
        target = jnp.where(routed[0:1] > 0, base + rank[0:1] - 1.0, -1.0)
        place = lax.broadcasted_iota(jnp.int32, (CROW, CTOK), 0).astype(F32)
        select = jnp.where(place == target, 1.0, 0.0)
        weight = jnp.sum(select * weight_row[0:1], axis=1, keepdims=True)
        select_t = select.T.astype(BF16)
        select = select.astype(BF16)
        for c in range(2 * NG):
            cols = slice((c % NG) * part, (c % NG + 1) * part)
            picked = dot(select, buf[kind, rows, c * part : (c + 1) * part])
            rows_all[c // NG, packed, cols] = picked.astype(BF16)

        combine_grad = jnp.zeros((CROW, 1), F32)
        for f in range(2):
            cols = slice(f * fhalf, (f + 1) * fhalf)
            x_rows = rows_all[0, packed, :]
            pre_gate = dot(x_rows, wg[:, cols])
            pre_up = dot(x_rows, wu[:, cols])
            back = dot(rows_all[1, packed, :], wd[cols, :], ((1,), (1,)))
            sigmoid = jax.nn.sigmoid(pre_gate)
            activation = pre_gate * sigmoid
            derivative = sigmoid * (1.0 + pre_gate * (1.0 - sigmoid))
            hidden = activation * pre_up
            combine_grad = combine_grad + jnp.sum(hidden * back, axis=1, keepdims=True)
            back = back * weight
            gate_rows = back * pre_up * derivative
            up_rows = back * activation
            pair[0, :, cols] = gate_rows.astype(BF16)
            pair[1, :, cols] = up_rows.astype(BF16)
            rows_t[0, cols, packed] = gate_rows.T.astype(BF16)
            rows_t[1, cols, packed] = up_rows.T.astype(BF16)
            rows_t[2, cols, packed] = (hidden * weight).T.astype(BF16)

        for c in range(NG):
            cols = slice(c * part, (c + 1) * part)
            row_grad = dot(pair[0], wg[cols, :], ((1,), (1,)))
            row_grad = row_grad + dot(pair[1], wu[cols, :], ((1,), (1,)))
            grads[kind, rows, cols] = dot(select_t, row_grad.astype(BF16)).astype(BF16)
        lanes = lax.broadcasted_iota(jnp.int32, (CROW, LANES), 1)
        spread = jnp.where(lanes == me, combine_grad, 0.0).astype(BF16)
        grads[kind, rows, width:grad_width] = dot(select_t, spread).astype(BF16)
        return rows

    def round_body(step, carry):
        kind = step % 2
        for c in range(2):
            for r, plan in plans[c].items():
                pl.when((step == r) & (core == c))(plan)

        @pl.when(kind != core)
        def _():
            def wait_block(i, carry):
                slot = (step // 2) * CHUNK + i
                pltpu.make_async_remote_copy(
                    src_ref=buf.at[kind, pl.ds(pl.multiple_of(slot * TOK, TOK), TOK)],
                    dst_ref=buf.at[kind, pl.ds(pl.multiple_of(slot * TOK, TOK), TOK)],
                    send_sem=core_send.at[slot],
                    recv_sem=ag_recv.at[(kind * BLOCKS + slot) * 2],
                    device_id=sibling,
                    device_id_type=MESH,
                ).wait_recv()
                return carry

            lax.fori_loop(0, CHUNK, wait_block, 0)

        @pl.when(step == 0)
        def _():
            for load in loads[2:]:
                load.wait()

        rows = chunk(step, kind)

        @pl.when(kind != core)
        def _():
            pair_copy(kind, rows).start()

        return carry

    lax.fori_loop(0, ROUNDS, round_body, 0)

    def tile(index, mat, half):
        left = rows_t[mat, half * fhalf : (half + 1) * fhalf, :]
        cols = pl.ds(pl.multiple_of(index * part, part), part)
        return dot(left, rows_all[0 if mat < 2 else 1, :, cols])

    def y_copy(source, step, way, mat):
        index = (step * 2 + way) * 3 + mat
        return pltpu.make_async_remote_copy(
            src_ref=source,
            dst_ref=yrecv.at[index],
            send_sem=y_send.at[index],
            recv_sem=y_recv.at[index],
            device_id=y_next if way == 0 else y_prev,
            device_id_type=MESH,
        )

    y_sent = []

    def y_task(step, mat):
        for way in range(2):
            shift = NG - 1 - step if way == 0 else 1 + step
            term = tile((group + shift) % NG, mat, way)
            if step == 0:
                source = ysend.at[way * 3 + mat]
                source[...] = term.astype(BF16)
            else:
                source = yrecv.at[((step - 1) * 2 + way) * 3 + mat]
                y_copy(source, step - 1, way, mat).wait_recv()
                term = term + source[...].astype(F32)
                if step < NG - 1:
                    source[...] = term.astype(BF16)
            if step < NG - 1:
                copy = y_copy(source, step, way, mat)
                copy.start()
                y_sent.append(copy)
            else:
                cols = slice(way * fhalf, (way + 1) * fhalf)
                if mat == 0:
                    o_gate[:, cols] = term.T.astype(BF16)
                elif mat == 1:
                    o_up[:, cols] = term.T.astype(BF16)
                else:
                    o_down[cols, :] = term.astype(BF16)

    def rows_of(ox, oz):
        a, b = slot_of(0, ox, oz), slot_of(1, ox, oz)
        return pl.multiple_of((a + (b - a) * core) * TOK, TOK)

    def block(ox, oz, half=None):
        first = rows_of(ox, oz)
        if half is None:
            return grads.at[core, pl.ds(first, TOK)]
        return grads.at[core, pl.ds(pl.multiple_of(first + half * HALF, HALF), HALF)]

    def push(source, target, send_sem, recv_sem, other):
        return pltpu.make_async_remote_copy(
            src_ref=source,
            dst_ref=target,
            send_sem=send_sem,
            recv_sem=recv_sem,
            device_id=other,
            device_id_type=MESH,
        )

    def far_copy(zi):
        oz = ZO[zi]
        other = x_prev if zi % 2 == 0 else x_next
        return push(block(2, oz), xfar.at[zi], xf_send.at[zi], xf_recv.at[zi], other)

    def near_copy(side, zi):
        oz = ZO[zi]
        index = side * NZ + zi
        other = x_prev if side == 0 else x_next
        return push(
            block(1 - 2 * side, oz), xnear.at[index], xn_send.at[index], xn_recv.at[index], other
        )

    def z_copy(side, k):
        sign = 1 - 2 * side
        other = z_prev if side == 0 else z_next
        index = side * 4 + k - 1
        target = znear.at[index]
        half = None
        if k == 4:
            half = side
            target = znear.at[index, pl.ds(side * HALF, HALF)]
        oz = 4 if k == 4 else sign * k
        return push(block(0, oz, half), target, z_send.at[index], z_recv.at[index], other)

    rs_sent = []

    def go(copy):
        copy.start()
        rs_sent.append(copy)

    def pair_sums():
        def body(i, carry):
            rows = pl.ds(pl.multiple_of(i * CTOK, CTOK), CTOK)
            copy = pair_copy(core, rows)
            copy.wait_recv()

            def piece(j, inner):
                part_rows = pl.ds(pl.multiple_of(i * CTOK + j * TOK, TOK), TOK)
                total = grads[core, part_rows, :].astype(F32) + sib[part_rows, :].astype(F32)
                grads[core, part_rows, :] = total.astype(BF16)
                return inner

            return lax.fori_loop(0, CHUNK, piece, carry)

        lax.fori_loop(0, BLOCKS // CHUNK, body, 0)

    zi_order = (7, 5, 6, 3, 4, 1, 2, 0)

    def x_start():
        for zi in zi_order:
            go(far_copy(zi))
        for zi in zi_order:
            go(near_copy(1 if zi % 2 == 0 else 0, zi))

    def x_add(zis):
        for zi in zis:
            side = 0 if zi % 2 == 0 else 1
            far_copy(zi).wait_recv()
            mine = block(1 - 2 * side, ZO[zi])
            mine[...] = (mine[...].astype(F32) + xfar[zi].astype(F32)).astype(BF16)
            go(near_copy(side, zi))

    def x_total(oz):
        zi = ZO.index(oz)
        near_copy(0, zi).wait_recv()
        near_copy(1, zi).wait_recv()
        mine = block(0, oz)
        return mine[...].astype(F32) + xnear[zi].astype(F32) + xnear[NZ + zi].astype(F32)

    def z_task(oz):
        total = x_total(oz)
        if oz == 4:
            block(0, oz)[...] = total.astype(BF16)
            go(z_copy(0, 4))
            go(z_copy(1, 4))
            return
        side = 0 if oz > 0 else 1
        k = abs(oz)
        index = side * 4 + k
        z_copy(side, k + 1).wait_recv()
        if k == 3:
            block(0, oz)[...] = total.astype(BF16)
            mine = block(0, oz, side)
            got = znear[index, side * HALF : (side + 1) * HALF, :]
            mine[...] = (mine[...].astype(F32) + got.astype(F32)).astype(BF16)
        else:
            block(0, oz)[...] = (total + znear[index].astype(F32)).astype(BF16)
        go(z_copy(side, k))

    def z_final():
        total = x_total(0)
        z_copy(0, 1).wait_recv()
        z_copy(1, 1).wait_recv()
        total = total + znear[0].astype(F32) + znear[4].astype(F32)
        o_tokens[...] = total[:, :width].astype(BF16)
        by_expert = total[:, width:grad_width]
        column = lax.broadcasted_iota(jnp.int32, o_combine.shape, 1)
        out = jnp.zeros(o_combine.shape, F32)
        for k in range(o_combine.shape[1]):
            value = jnp.sum(
                jnp.where(expert_ids[:, k : k + 1] == lane_iota, by_expert, 0.0),
                axis=1,
                keepdims=True,
            )
            out = out + jnp.where(column == k, value, 0.0)
        o_combine[...] = out.astype(BF16)

    for mat in range(3):
        y_task(0, mat)
    pair_sums()
    x_start()
    y_task(1, 0)
    y_task(1, 1)
    x_add(zi_order[:4])
    y_task(1, 2)
    x_add(zi_order[4:])
    y_task(2, 0)
    y_task(2, 1)
    z_task(4)
    z_task(3)
    z_task(-3)
    y_task(2, 2)
    z_task(2)
    z_task(-2)
    z_task(1)
    z_task(-1)
    y_task(3, 0)
    z_final()
    y_task(3, 1)
    y_task(3, 2)

    for kind in range(2):

        @pl.when(core == kind)
        def _(kind=kind):
            for (target, half), (source, other) in hops[kind].items():
                hop(kind, source, target, other, half).wait_send()
            for offset in shares[kind]:
                across(kind, slot_of(kind, *offset)).wait_send()

    def pair_done(i, carry):
        pair_copy(1 - core, pl.ds(pl.multiple_of(i * CTOK, CTOK), CTOK)).wait_send()
        return carry

    lax.fori_loop(0, BLOCKS // CHUNK, pair_done, 0)
    for copy in y_sent + rs_sent:
        copy.wait_send()


def shards(tokens, grad_out, combine, expert_ids, w_gate, w_up, w_down):
    tok, width = tokens.shape
    top = expert_ids.shape[1]
    ff = w_gate.shape[2]
    part = width // NG
    slots = BLOCKS * TOK
    picked = ROUNDS * CROW
    gw = width + LANES
    any_spec = pl.BlockSpec(memory_space=pl.ANY)
    vmem_spec = pl.BlockSpec(memory_space=pltpu.VMEM)
    dma = pltpu.SemaphoreType.DMA
    results = pl.pallas_call(
        kernel,
        out_shape=(
            jax.ShapeDtypeStruct((tok, width), BF16),
            jax.ShapeDtypeStruct((tok, top), BF16),
            jax.ShapeDtypeStruct((part, ff), BF16),
            jax.ShapeDtypeStruct((part, ff), BF16),
            jax.ShapeDtypeStruct((ff, part), BF16),
        ),
        in_specs=[any_spec, any_spec, vmem_spec, vmem_spec, any_spec, any_spec, any_spec],
        out_specs=[vmem_spec] * 5,
        scratch_shapes=[
            pltpu.VMEM((2, slots, 2 * width + LANES), BF16),
            pltpu.VMEM((width, ff), BF16),
            pltpu.VMEM((width, ff), BF16),
            pltpu.VMEM((ff, width), BF16),
            pltpu.VMEM((2, picked, width), BF16),
            pltpu.VMEM((3, ff, picked), BF16),
            pltpu.VMEM((2, CROW, ff), BF16),
            pltpu.VMEM((2, slots, gw), BF16),
            pltpu.VMEM((slots, gw), BF16),
            pltpu.VMEM((6, ff // 2, part), BF16),
            pltpu.VMEM((18, ff // 2, part), BF16),
            pltpu.VMEM((NZ, tok, gw), BF16),
            pltpu.VMEM((2 * NZ, tok, gw), BF16),
            pltpu.VMEM((8, tok, gw), BF16),
            dma((5,)),
            dma((4 * BLOCKS,)),
            dma((4 * BLOCKS,)),
            dma((BLOCKS,)),
            dma((BLOCKS // CHUNK,)),
            dma((BLOCKS // CHUNK,)),
            dma((18,)),
            dma((18,)),
            dma((NZ,)),
            dma((NZ,)),
            dma((2 * NZ,)),
            dma((2 * NZ,)),
            dma((8,)),
            dma((8,)),
        ],
        compiler_params=pltpu.CompilerParams(
            collective_id=0, has_side_effects=True, vmem_limit_bytes=63 << 20
        ),
    )(tokens, grad_out, combine, expert_ids, w_gate[0], w_up[0], w_down[0])
    g_tokens, g_combine, g_gate, g_up, g_down = results
    return g_tokens, g_combine, g_gate[None], g_up[None], g_down[None]


def solution(mesh):
    rows = P(("grp", "ep"), None)
    expert = P("ep", None, None)
    return jax.shard_map(
        shards,
        mesh=mesh,
        in_specs=(rows, rows, rows, rows, expert, expert, expert),
        out_specs=(rows, rows, P("ep", "grp", None), P("ep", "grp", None), P("ep", None, "grp")),
        check_vma=False,
    )
```

```python
import functools

import jax
import jax.numpy as jnp
from jax import lax
from jax.experimental import pallas as pl
from jax.experimental.pallas import tpu as pltpu
from jax.sharding import PartitionSpec as P

MESH = pl.DeviceIdType.MESH
F32 = jnp.float32
BF16 = jnp.bfloat16

NX, NZ, NG = 4, 8, 4
TOK = 32
HALF = TOK // 2
CAP = 16
LANES = 128
XO = (0, 1, -1, 2)
ZO = (0, 1, -1, 2, -2, 3, -3, 4)
BLOCKS = NX * NZ
CHUNK = 8
CTOK = CHUNK * TOK
CROW = CHUNK * CAP
ROUNDS = BLOCKS // CHUNK


ORDER = (
    (
        *((0, 0), (1, 0), (-1, 0), (2, 0), (0, 1), (0, -1), (1, 1), (1, -1)),
        *((-1, 1), (-1, -1), (2, 1), (2, -1), (0, 2), (0, -2), (1, 2), (1, -2)),
        *((-1, 2), (-1, -2), (2, 2), (2, -2), (0, 3), (0, -3), (1, 3), (1, -3)),
        *((-1, 3), (-1, -3), (2, 3), (2, -3), (-1, 4), (1, 4), (0, 4), (2, 4)),
    ),
    (
        *((0, 0), (0, 1), (0, -1), (1, 0), (-1, 0), (0, 2), (0, -2), (1, 1)),
        *((-1, 1), (1, -1), (-1, -1), (0, 3), (0, -3), (2, 0), (1, 2), (-1, 2)),
        *((1, -2), (-1, -2), (0, 4), (2, 1), (2, -1), (1, 3), (-1, 3), (1, -3)),
        *((-1, -3), (1, 4), (-1, 4), (2, 2), (2, -2), (2, 3), (2, -3), (2, 4)),
    ),
)


def slot_of(kind, ox, oz):
    return ORDER[kind].index((ox, oz))


def children(kind, ox, oz, half):
    found = []
    if kind == 0 and oz == 0 or kind == 1:
        if ox == 0:
            found += [((1, oz), 0), ((-1, oz), 1)]
        elif (ox, half) == (1, 0):
            found.append(((2, oz), 0))
        elif (ox, half) == (-1, 1):
            found.append(((2, oz), 1))
    elif (ox, half) == (1, 0) and oz in (-2, 3, -3, 4):
        found.append(((2, oz), 0))
    elif (ox, half) == (-1, 1) and oz in (2, 3, -3, 4):
        found.append(((2, oz), 1))
    along_z = ox == 0 if kind == 1 else ox != 2 or oz == 0 or (oz, half) in ((1, 0), (-1, 1))
    if along_z:
        if oz == 0:
            found += [((ox, 1), 2), ((ox, -1), 3)]
        elif oz in (1, 2) or (oz, half) == (3, 0):
            found.append(((ox, oz + 1), 2))
        elif oz in (-1, -2):
            found.append(((ox, oz - 1), 3))
        elif (oz, half) == (-3, 1):
            found.append(((ox, 4), 3))
    return found


def dot(left, right, dims=((1,), (0,))):
    return lax.dot_general(left, right, (dims, ((), ())), preferred_element_type=F32)


def identity(size):
    row = lax.broadcasted_iota(jnp.int32, (size, size), 0)
    col = lax.broadcasted_iota(jnp.int32, (size, size), 1)
    return (row == col).astype(F32).astype(BF16)


def kernel(
    tokens,
    grad_out,
    combine,
    expert_ids,
    w_gate,
    w_up,
    w_down,
    o_tokens,
    o_combine,
    o_gate,
    o_up,
    o_down,
    buf,
    wg,
    wu,
    wd,
    rows_all,
    rows_t,
    pair,
    grads,
    sib,
    ysend,
    yrecv,
    xfar,
    xnear,
    znear,
    in_sem,
    ag_send,
    ag_recv,
    core_send,
    sib_send,
    sib_recv,
    y_send,
    y_recv,
    xf_send,
    xf_recv,
    xn_send,
    xn_recv,
    z_send,
    z_recv,
):
    width = tokens.shape[1]
    hidden_width = w_gate.shape[1]
    part = width // NG
    fhalf = hidden_width // 2
    grad_width = width + LANES
    me = lax.axis_index("ep")
    group = lax.axis_index("grp")
    core = me % 2
    zpos = (me // 2) % NZ
    xpos = me // (2 * NZ)

    def at(dx, dz):
        return {"ep": (((xpos + dx + NX) % NX) * NZ + (zpos + dz + NZ) % NZ) * 2 + core}

    sibling = {"ep": me + 1 - 2 * core}
    y_next = {"grp": (group + 1) % NG}
    y_prev = {"grp": (group + NG - 1) % NG}
    x_next, x_prev, z_next, z_prev = at(1, 0), at(-1, 0), at(0, 1), at(0, -1)

    barrier = pltpu.get_barrier_semaphore()
    for other in (sibling, x_next, x_prev, z_next, z_prev, y_next, y_prev):
        pl.semaphore_signal(barrier, inc=1, device_id=other, device_id_type=MESH)

    loads = [
        pltpu.make_async_copy(tokens, buf.at[core, pl.ds(0, TOK), pl.ds(0, width)], in_sem.at[0]),
        pltpu.make_async_copy(
            grad_out, buf.at[core, pl.ds(0, TOK), pl.ds(width, width)], in_sem.at[1]
        ),
        pltpu.make_async_copy(w_gate, wg, in_sem.at[2]),
        pltpu.make_async_copy(w_up, wu, in_sem.at[3]),
        pltpu.make_async_copy(w_down, wd, in_sem.at[4]),
    ]
    for load in loads:
        load.start()
    top = expert_ids.shape[0]
    expert_iota = lax.broadcasted_iota(jnp.int32, (LANES, TOK), 0)
    weights = combine[...].astype(F32)
    table = jnp.zeros((LANES, TOK), F32)
    for k in range(top):
        named = expert_ids[k : k + 1, :] == expert_iota
        table = table + jnp.where(named, weights[k : k + 1, :], 0.0)
    table = dot(identity(TOK), table.astype(BF16), ((1,), (1,)))
    buf[core, 0:TOK, 2 * width : 2 * width + LANES] = table.astype(BF16)
    loads[0].wait()
    loads[1].wait()
    pl.semaphore_wait(barrier, 7)

    hops, shares = ({}, {}), ({}, {})

    def span(slot, half):
        if half is None:
            return pl.ds(slot * TOK, TOK)
        return pl.ds(slot * TOK + half * HALF, HALF)

    def hop(kind, source, target, other, half):
        a, b = slot_of(kind, *source), slot_of(kind, *target)
        index = (kind * BLOCKS + b) * 2 + half
        return pltpu.make_async_remote_copy(
            src_ref=buf.at[kind, span(a, half)],
            dst_ref=buf.at[kind, span(b, half)],
            send_sem=ag_send.at[index],
            recv_sem=ag_recv.at[index],
            device_id=other,
            device_id_type=MESH,
        )

    def across(kind, slot):
        return pltpu.make_async_remote_copy(
            src_ref=buf.at[kind, span(slot, None)],
            dst_ref=buf.at[kind, span(slot, None)],
            send_sem=core_send.at[slot],
            recv_sem=ag_recv.at[(kind * BLOCKS + slot) * 2],
            device_id=sibling,
            device_id_type=MESH,
        )

    def forward(kind, offset, half):
        for target, way in children(kind, *offset, half):
            other = (x_next, x_prev, z_next, z_prev)[way]
            hop(kind, offset, target, other, half).start()
            hops[kind][target, half] = offset, other

    def share(kind, offset):
        across(kind, slot_of(kind, *offset)).start()
        shares[kind][offset] = True

    def serve(kind, offset):
        for half in range(2):
            if offset != (0, 0):
                hop(kind, offset, offset, z_next, half).wait_recv()
            forward(kind, offset, half)
        share(kind, offset)

    def serve_all(step, kind, offsets):
        @pl.when((step == 0) & (core == kind))
        def _():
            for offset in offsets:
                serve(kind, offset)

    def service(step, place):
        for kind in range(2):
            for r in range(1, ROUNDS):

                @pl.when((step == r - 1) & (core == kind))
                def _(kind=kind, r=r):
                    serve(kind, ORDER[kind][r * CHUNK + place])

    def pair_copy(kind, rows, step):
        return pltpu.make_async_remote_copy(
            src_ref=grads.at[kind, rows],
            dst_ref=sib.at[rows],
            send_sem=sib_send.at[step],
            recv_sem=sib_recv.at[step],
            device_id=sibling,
            device_id_type=MESH,
        )

    def chunk(step):
        rows = pl.ds(pl.multiple_of(step * CTOK, CTOK), CTOK)
        first = pl.multiple_of(step * 2 * CROW, 2 * CROW)
        packed = pl.ds(first, 2 * CROW)
        pick = (lax.broadcasted_iota(jnp.int32, (CAP, LANES), 1) == me).astype(F32).astype(BF16)
        row_id = lax.broadcasted_iota(jnp.int32, (CTOK, CTOK), 0)
        col_id = lax.broadcasted_iota(jnp.int32, (CTOK, CTOK), 1)
        upto = (row_id <= col_id) & (row_id // TOK == col_id // TOK)
        upto = upto.astype(F32).astype(BF16)
        base = (lax.broadcasted_iota(jnp.int32, (1, CTOK), 1) // TOK * CAP).astype(F32)
        place = lax.broadcasted_iota(jnp.int32, (CROW, CTOK), 0).astype(F32)
        weight_parts, back_select = [], []
        for kind in range(2):
            table = buf[kind, rows, 2 * width : 2 * width + LANES]
            weight_row = dot(pick, table, ((1,), (1,)))
            routed = jnp.where(weight_row > 0, 1.0, 0.0)
            rank = dot(routed.astype(BF16), upto)
            target = jnp.where(routed[0:1] > 0, base + rank[0:1] - 1.0, -1.0)
            select = jnp.where(place == target, 1.0, 0.0)
            weight_parts.append(jnp.sum(select * weight_row[0:1], axis=1, keepdims=True))
            back_select.append(select.T.astype(BF16))
            select = select.astype(BF16)
            own = pl.ds(pl.multiple_of(first + kind * CROW, CROW), CROW)
            for c in range(2 * NG):
                cols = slice((c % NG) * part, (c % NG + 1) * part)
                picked = dot(select, buf[kind, rows, c * part : (c + 1) * part])
                rows_all[c // NG, own, cols] = picked.astype(BF16)
            service(step, kind)
        weight = jnp.concatenate(weight_parts, axis=0)

        combine_grad = jnp.zeros((2 * CROW, 1), F32)
        for f in range(2):
            cols = slice(f * fhalf, (f + 1) * fhalf)
            x_rows = rows_all[0, packed, :]
            pre_gate = dot(x_rows, wg[:, cols])
            pre_up = dot(x_rows, wu[:, cols])
            back = dot(rows_all[1, packed, :], wd[cols, :], ((1,), (1,)))
            sigmoid = jax.nn.sigmoid(pre_gate)
            activation = pre_gate * sigmoid
            derivative = sigmoid * (1.0 + pre_gate * (1.0 - sigmoid))
            hidden = activation * pre_up
            combine_grad = combine_grad + jnp.sum(hidden * back, axis=1, keepdims=True)
            back = back * weight
            gate_rows = back * pre_up * derivative
            up_rows = back * activation
            pair[0, :, cols] = gate_rows.astype(BF16)
            pair[1, :, cols] = up_rows.astype(BF16)
            rows_t[0, cols, packed] = gate_rows.T.astype(BF16)
            rows_t[1, cols, packed] = up_rows.T.astype(BF16)
            rows_t[2, cols, packed] = (hidden * weight).T.astype(BF16)
            service(step, 2 + f)

        for c in range(NG):
            cols = slice(c * part, (c + 1) * part)
            row_grad = dot(pair[0], wg[cols, :], ((1,), (1,)))
            row_grad = row_grad + dot(pair[1], wu[cols, :], ((1,), (1,)))
            row_grad = row_grad.astype(BF16)
            for kind in range(2):
                mine = row_grad[kind * CROW : (kind + 1) * CROW]
                grads[kind, rows, cols] = dot(back_select[kind], mine).astype(BF16)
            service(step, 4 + c)
        lanes = lax.broadcasted_iota(jnp.int32, (2 * CROW, LANES), 1)
        spread = jnp.where(lanes == me, combine_grad, 0.0).astype(BF16)
        for kind in range(2):
            mine = spread[kind * CROW : (kind + 1) * CROW]
            grads[kind, rows, width:grad_width] = dot(back_select[kind], mine).astype(BF16)

    def pair_sum(step):
        first = pl.multiple_of(step * CTOK, CTOK)
        pair_copy(core, pl.ds(first, CTOK), step).wait_recv()

        def piece(j, carry):
            rows = pl.ds(pl.multiple_of(first + j * TOK, TOK), TOK)
            total = grads[core, rows, :].astype(F32) + sib[rows, :].astype(F32)
            grads[core, rows, :] = total.astype(BF16)
            return carry

        lax.fori_loop(0, CHUNK, piece, 0)

    def round_body(step, carry):
        for kind in range(2):
            serve_all(step, kind, ORDER[kind][:CHUNK])

        def wait_block(i, inner):
            slot = step * CHUNK + i
            rows = pl.ds(pl.multiple_of(slot * TOK, TOK), TOK)
            pltpu.make_async_remote_copy(
                src_ref=buf.at[1 - core, rows],
                dst_ref=buf.at[1 - core, rows],
                send_sem=core_send.at[slot],
                recv_sem=ag_recv.at[((1 - core) * BLOCKS + slot) * 2],
                device_id=sibling,
                device_id_type=MESH,
            ).wait_recv()
            return inner

        lax.fori_loop(0, CHUNK, wait_block, 0)

        @pl.when(step == 0)
        def _():
            for load in loads[2:]:
                load.wait()

        chunk(step)
        pair_copy(1 - core, pl.ds(pl.multiple_of(step * CTOK, CTOK), CTOK), step).start()

        @pl.when(step > 0)
        def _():
            pair_sum(step - 1)

        return carry

    lax.fori_loop(0, ROUNDS, round_body, 0)

    def tile(index, mat, half):
        left = rows_t[mat, half * fhalf : (half + 1) * fhalf, :]
        cols = pl.ds(pl.multiple_of(index * part, part), part)
        return dot(left, rows_all[0 if mat < 2 else 1, :, cols])

    def y_copy(source, step, way, mat):
        index = (step * 2 + way) * 3 + mat
        return pltpu.make_async_remote_copy(
            src_ref=source,
            dst_ref=yrecv.at[index],
            send_sem=y_send.at[index],
            recv_sem=y_recv.at[index],
            device_id=y_next if way == 0 else y_prev,
            device_id_type=MESH,
        )

    y_sent = []

    def y_task(step, mat):
        for way in range(2):
            shift = NG - 1 - step if way == 0 else 1 + step
            term = tile((group + shift) % NG, mat, way)
            if step == 0:
                source = ysend.at[way * 3 + mat]
                source[...] = term.astype(BF16)
            else:
                source = yrecv.at[((step - 1) * 2 + way) * 3 + mat]
                y_copy(source, step - 1, way, mat).wait_recv()
                term = term + source[...].astype(F32)
                if step < NG - 1:
                    source[...] = term.astype(BF16)
            if step < NG - 1:
                copy = y_copy(source, step, way, mat)
                copy.start()
                y_sent.append(copy)
            else:
                cols = slice(way * fhalf, (way + 1) * fhalf)
                if mat == 0:
                    o_gate[:, cols] = term.T.astype(BF16)
                elif mat == 1:
                    o_up[:, cols] = term.T.astype(BF16)
                else:
                    o_down[cols, :] = term.astype(BF16)

    def rows_of(ox, oz):
        a, b = slot_of(0, ox, oz), slot_of(1, ox, oz)
        return pl.multiple_of((a + (b - a) * core) * TOK, TOK)

    def block(ox, oz, half=None):
        first = rows_of(ox, oz)
        if half is None:
            return grads.at[core, pl.ds(first, TOK)]
        return grads.at[core, pl.ds(pl.multiple_of(first + half * HALF, HALF), HALF)]

    def push(source, target, send_sem, recv_sem, other):
        return pltpu.make_async_remote_copy(
            src_ref=source,
            dst_ref=target,
            send_sem=send_sem,
            recv_sem=recv_sem,
            device_id=other,
            device_id_type=MESH,
        )

    def far_copy(zi):
        oz = ZO[zi]
        other = x_prev if zi % 2 == 0 else x_next
        return push(block(2, oz), xfar.at[zi], xf_send.at[zi], xf_recv.at[zi], other)

    def near_copy(side, zi):
        oz = ZO[zi]
        index = side * NZ + zi
        other = x_prev if side == 0 else x_next
        return push(
            block(1 - 2 * side, oz), xnear.at[index], xn_send.at[index], xn_recv.at[index], other
        )

    def z_copy(side, k):
        sign = 1 - 2 * side
        other = z_prev if side == 0 else z_next
        index = side * 4 + k - 1
        target = znear.at[index]
        half = None
        if k == 4:
            half = side
            target = znear.at[index, pl.ds(side * HALF, HALF)]
        oz = 4 if k == 4 else sign * k
        return push(block(0, oz, half), target, z_send.at[index], z_recv.at[index], other)

    rs_sent = []

    def go(copy):
        copy.start()
        rs_sent.append(copy)

    zi_order = (7, 5, 6, 3, 4, 1, 2, 0)

    def x_start():
        for zi in zi_order:
            go(far_copy(zi))
        for zi in zi_order:
            go(near_copy(1 if zi % 2 == 0 else 0, zi))

    def x_add(zis):
        for zi in zis:
            side = 0 if zi % 2 == 0 else 1
            far_copy(zi).wait_recv()
            mine = block(1 - 2 * side, ZO[zi])
            mine[...] = (mine[...].astype(F32) + xfar[zi].astype(F32)).astype(BF16)
            go(near_copy(side, zi))

    def x_total(oz):
        zi = ZO.index(oz)
        near_copy(0, zi).wait_recv()
        near_copy(1, zi).wait_recv()
        mine = block(0, oz)
        return mine[...].astype(F32) + xnear[zi].astype(F32) + xnear[NZ + zi].astype(F32)

    def z_task(oz):
        total = x_total(oz)
        if oz == 4:
            block(0, oz)[...] = total.astype(BF16)
            go(z_copy(0, 4))
            go(z_copy(1, 4))
            return
        side = 0 if oz > 0 else 1
        k = abs(oz)
        index = side * 4 + k
        z_copy(side, k + 1).wait_recv()
        if k == 3:
            block(0, oz)[...] = total.astype(BF16)
            mine = block(0, oz, side)
            got = znear[index, side * HALF : (side + 1) * HALF, :]
            mine[...] = (mine[...].astype(F32) + got.astype(F32)).astype(BF16)
        else:
            block(0, oz)[...] = (total + znear[index].astype(F32)).astype(BF16)
        go(z_copy(side, k))

    def z_final():
        total = x_total(0)
        z_copy(0, 1).wait_recv()
        z_copy(1, 1).wait_recv()
        total = total + znear[0].astype(F32) + znear[4].astype(F32)
        o_tokens[...] = total[:, :width].astype(BF16)
        by_expert = total[:, width:grad_width].astype(BF16)
        by_expert = dot(identity(LANES), by_expert, ((1,), (1,)))
        for k in range(top):
            named = expert_ids[k : k + 1, :] == expert_iota
            value = jnp.sum(jnp.where(named, by_expert, 0.0), axis=0, keepdims=True)
            o_combine[k : k + 1, :] = value.astype(BF16)

    for mat in range(3):
        y_task(0, mat)
    pair_sum(ROUNDS - 1)
    x_start()
    y_task(1, 0)
    y_task(1, 1)
    x_add(zi_order[:4])
    y_task(1, 2)
    x_add(zi_order[4:])
    y_task(2, 0)
    y_task(2, 1)
    z_task(4)
    z_task(3)
    z_task(-3)
    y_task(2, 2)
    z_task(2)
    z_task(-2)
    z_task(1)
    z_task(-1)
    y_task(3, 0)
    z_final()
    y_task(3, 1)
    y_task(3, 2)

    for kind in range(2):

        @pl.when(core == kind)
        def _(kind=kind):
            for (target, half), (source, other) in hops[kind].items():
                hop(kind, source, target, other, half).wait_send()
            for offset in shares[kind]:
                across(kind, slot_of(kind, *offset)).wait_send()

    def pair_done(i, carry):
        pair_copy(1 - core, pl.ds(pl.multiple_of(i * CTOK, CTOK), CTOK), i).wait_send()
        return carry

    lax.fori_loop(0, BLOCKS // CHUNK, pair_done, 0)
    for copy in y_sent + rs_sent:
        copy.wait_send()


def hand_out(*refs):
    sources, targets, held, sems = refs[:5], refs[5:10], refs[10:15], refs[15]
    taken = [pltpu.make_async_copy(sources[i], held[i], sems.at[i]) for i in range(5)]
    given = [pltpu.make_async_copy(held[i], targets[i], sems.at[5 + i]) for i in range(5)]
    for copy in taken:
        copy.start()
    for before, after in zip(taken, given):
        before.wait()
        after.start()
    for copy in given:
        copy.wait()


def shards(tokens, grad_out, combine, expert_ids, w_gate, w_up, w_down):
    tok, width = tokens.shape
    top = expert_ids.shape[1]
    ff = w_gate.shape[2]
    part = width // NG
    slots = BLOCKS * TOK
    picked = 2 * ROUNDS * CROW
    gw = width + LANES
    any_spec = pl.BlockSpec(memory_space=pl.ANY)
    vmem_spec = pl.BlockSpec(memory_space=pltpu.VMEM)
    dma = pltpu.SemaphoreType.DMA
    results = pl.pallas_call(
        kernel,
        out_shape=(
            jax.ShapeDtypeStruct((tok, width), BF16),
            jax.ShapeDtypeStruct((top, tok), BF16),
            jax.ShapeDtypeStruct((part, ff), BF16),
            jax.ShapeDtypeStruct((part, ff), BF16),
            jax.ShapeDtypeStruct((ff, part), BF16),
        ),
        in_specs=[any_spec, any_spec, vmem_spec, vmem_spec, any_spec, any_spec, any_spec],
        out_specs=[vmem_spec] * 5,
        scratch_shapes=[
            pltpu.VMEM((2, slots, 2 * width + LANES), BF16),
            pltpu.VMEM((width, ff), BF16),
            pltpu.VMEM((width, ff), BF16),
            pltpu.VMEM((ff, width), BF16),
            pltpu.VMEM((2, picked, width), BF16),
            pltpu.VMEM((3, ff, picked), BF16),
            pltpu.VMEM((2, 2 * CROW, ff), BF16),
            pltpu.VMEM((2, slots, gw), BF16),
            pltpu.VMEM((slots, gw), BF16),
            pltpu.VMEM((6, ff // 2, part), BF16),
            pltpu.VMEM((18, ff // 2, part), BF16),
            pltpu.VMEM((NZ, tok, gw), BF16),
            pltpu.VMEM((2 * NZ, tok, gw), BF16),
            pltpu.VMEM((8, tok, gw), BF16),
            dma((5,)),
            dma((4 * BLOCKS,)),
            dma((4 * BLOCKS,)),
            dma((BLOCKS,)),
            dma((BLOCKS // CHUNK,)),
            dma((BLOCKS // CHUNK,)),
            dma((18,)),
            dma((18,)),
            dma((NZ,)),
            dma((NZ,)),
            dma((2 * NZ,)),
            dma((2 * NZ,)),
            dma((8,)),
            dma((8,)),
        ],
        compiler_params=pltpu.CompilerParams(
            collective_id=0, has_side_effects=True, vmem_limit_bytes=63 << 20
        ),
    )(tokens, grad_out, combine.T, expert_ids.T, w_gate[0], w_up[0], w_down[0])
    results = pl.pallas_call(
        hand_out,
        out_shape=tuple(jax.ShapeDtypeStruct(r.shape, r.dtype) for r in results),
        in_specs=[any_spec] * 5,
        out_specs=[any_spec] * 5,
        scratch_shapes=[pltpu.VMEM(r.shape, r.dtype) for r in results] + [dma((10,))],
    )(*results)
    g_tokens, g_combine, g_gate, g_up, g_down = results
    return g_tokens, g_combine.T, g_gate[None], g_up[None], g_down[None]


def solution(mesh):
    rows = P(("grp", "ep"), None)
    expert = P("ep", None, None)
    return jax.shard_map(
        shards,
        mesh=mesh,
        in_specs=(rows, rows, rows, rows, expert, expert, expert),
        out_specs=(rows, rows, P("ep", "grp", None), P("ep", "grp", None), P("ep", None, "grp")),
        check_vma=False,
    )
```

```python
import functools

import jax
import jax.numpy as jnp
from jax import lax
from jax.experimental import pallas as pl
from jax.experimental.pallas import tpu as pltpu
from jax.sharding import PartitionSpec as P

MESH = pl.DeviceIdType.MESH
F32 = jnp.float32
BF16 = jnp.bfloat16

NX, NZ, NG = 4, 8, 4
TOK = 32
HALF = TOK // 2
CAP = 16
LANES = 128
XO = (0, 1, -1, 2)
ZO = (0, 1, -1, 2, -2, 3, -3, 4)
BLOCKS = NX * NZ
CHUNK = 8
CTOK = CHUNK * TOK
CROW = CHUNK * CAP
ROUNDS = BLOCKS // CHUNK


ORDER = (
    (
        *((0, 0), (1, 0), (0, 1), (1, -1), (0, -1), (0, 2), (-1, -1), (1, 1)),
        *((0, -2), (-1, -2), (0, 3), (1, 2), (0, -3), (2, 0), (-1, 1), (2, -1)),
        *((2, 1), (-1, -3), (-1, 0), (0, 4), (1, -2), (-1, 2), (1, 3), (2, 2)),
        *((2, -3), (-1, 3), (-1, 4), (1, 4), (2, 3), (2, -2), (1, -3), (2, 4)),
    ),
    (
        *((0, 0), (0, 1), (0, -1), (-1, 0), (0, 2), (-1, 1), (0, -2), (1, -1)),
        *((1, 1), (0, -3), (0, 3), (2, -1), (1, 0), (1, 2), (1, -2), (-1, -2)),
        *((-1, 2), (2, 1), (0, 4), (1, 3), (2, -2), (-1, 3), (-1, -1), (-1, -3)),
        *((1, -3), (2, 0), (2, 2), (-1, 4), (2, 3), (2, -3), (1, 4), (2, 4)),
    ),
)
WAYS = (
    (
        (-1, 0, 2, 3, 3, 2, 1, 2, 3, 3, 2, 2, 3, 0, 1, 1, 0, 3, 1, 2, 3, 2, 2, 0, 1, 1, 3, 2, 0, 2, 3, 0),
        (-1, 0, 2, 3, 3, 2, 1, 0, 3, 3, 2, 2, 3, 0, 1, 1, 0, 3, 1, 3, 0, 2, 0, 0, 1, 2, 3, 2, 0, 2, 1, 3),
    ),
    (
        (-1, 2, 3, 1, 2, 1, 3, 0, 0, 3, 2, 0, 2, 2, 0, 1, 1, 0, 2, 2, 1, 1, 0, 1, 3, 3, 2, 1, 0, 1, 3, 2),
        (-1, 2, 3, 1, 2, 1, 3, 0, 0, 3, 2, 0, 0, 0, 0, 1, 1, 1, 3, 0, 1, 2, 0, 1, 3, 3, 1, 1, 0, 0, 3, 1),
    ),
)
MOVES = ((1, 0), (-1, 0), (0, 1), (0, -1))


def slot_of(kind, ox, oz):
    return ORDER[kind].index((ox, oz))


def children(kind, ox, oz, half):
    found = []
    for target, way in zip(ORDER[kind], WAYS[kind][half]):
        dx, dz = MOVES[way]
        if way >= 0 and (target[0] - ox - dx) % NX == 0 and (target[1] - oz - dz) % NZ == 0:
            found.append((target, way))
    return found


def dot(left, right, dims=((1,), (0,))):
    return lax.dot_general(left, right, (dims, ((), ())), preferred_element_type=F32)


def identity(size):
    row = lax.broadcasted_iota(jnp.int32, (size, size), 0)
    col = lax.broadcasted_iota(jnp.int32, (size, size), 1)
    return (row == col).astype(F32).astype(BF16)


def kernel(
    tokens,
    grad_out,
    combine,
    expert_ids,
    w_gate,
    w_up,
    w_down,
    o_tokens,
    o_combine,
    o_gate,
    o_up,
    o_down,
    buf,
    wg,
    wu,
    wd,
    rows_all,
    rows_t,
    pair,
    back_select,
    spread,
    grads,
    sib,
    ysend,
    yrecv,
    xfar,
    xnear,
    znear,
    in_sem,
    ag_send,
    ag_recv,
    core_send,
    sib_send,
    sib_recv,
    y_send,
    y_recv,
    xf_send,
    xf_recv,
    xn_send,
    xn_recv,
    z_send,
    z_recv,
):
    width = tokens.shape[1]
    hidden_width = w_gate.shape[1]
    part = width // NG
    fhalf = hidden_width // 2
    grad_width = width + LANES
    me = lax.axis_index("ep")
    group = lax.axis_index("grp")
    core = me % 2
    zpos = (me // 2) % NZ
    xpos = me // (2 * NZ)

    def at(dx, dz):
        return {"ep": (((xpos + dx + NX) % NX) * NZ + (zpos + dz + NZ) % NZ) * 2 + core}

    sibling = {"ep": me + 1 - 2 * core}
    y_next = {"grp": (group + 1) % NG}
    y_prev = {"grp": (group + NG - 1) % NG}
    x_next, x_prev, z_next, z_prev = at(1, 0), at(-1, 0), at(0, 1), at(0, -1)

    barrier = pltpu.get_barrier_semaphore()
    for other in (sibling, x_next, x_prev, z_next, z_prev, y_next, y_prev):
        pl.semaphore_signal(barrier, inc=1, device_id=other, device_id_type=MESH)

    loads = [
        pltpu.make_async_copy(tokens, buf.at[core, pl.ds(0, TOK), pl.ds(0, width)], in_sem.at[0]),
        pltpu.make_async_copy(
            grad_out, buf.at[core, pl.ds(0, TOK), pl.ds(width, width)], in_sem.at[1]
        ),
        pltpu.make_async_copy(w_gate, wg, in_sem.at[2]),
        pltpu.make_async_copy(w_up, wu, in_sem.at[3]),
        pltpu.make_async_copy(w_down, wd, in_sem.at[4]),
    ]
    for load in loads:
        load.start()
    top = expert_ids.shape[0]
    expert_iota = lax.broadcasted_iota(jnp.int32, (LANES, TOK), 0)
    weights = combine[...].astype(F32)
    table = jnp.zeros((LANES, TOK), F32)
    for k in range(top):
        named = expert_ids[k : k + 1, :] == expert_iota
        table = table + jnp.where(named, weights[k : k + 1, :], 0.0)
    table = dot(identity(TOK), table.astype(BF16), ((1,), (1,)))
    buf[core, 0:TOK, 2 * width : 2 * width + LANES] = table.astype(BF16)
    loads[0].wait()
    loads[1].wait()
    pl.semaphore_wait(barrier, 7)

    hops, shares = ({}, {}), ({}, {})

    def span(slot, half):
        if half is None:
            return pl.ds(slot * TOK, TOK)
        return pl.ds(slot * TOK + half * HALF, HALF)

    def hop(kind, source, target, other, half):
        a, b = slot_of(kind, *source), slot_of(kind, *target)
        index = (kind * BLOCKS + b) * 2 + half
        return pltpu.make_async_remote_copy(
            src_ref=buf.at[kind, span(a, half)],
            dst_ref=buf.at[kind, span(b, half)],
            send_sem=ag_send.at[index],
            recv_sem=ag_recv.at[index],
            device_id=other,
            device_id_type=MESH,
        )

    def across(kind, slot):
        return pltpu.make_async_remote_copy(
            src_ref=buf.at[kind, span(slot, None)],
            dst_ref=buf.at[kind, span(slot, None)],
            send_sem=core_send.at[slot],
            recv_sem=ag_recv.at[(kind * BLOCKS + slot) * 2],
            device_id=sibling,
            device_id_type=MESH,
        )

    def forward(kind, offset, half):
        for target, way in children(kind, *offset, half):
            other = (x_next, x_prev, z_next, z_prev)[way]
            hop(kind, offset, target, other, half).start()
            hops[kind][target, half] = offset, other

    def share(kind, offset):
        across(kind, slot_of(kind, *offset)).start()
        shares[kind][offset] = True

    def serve(kind, offset):
        for half in range(2):
            if offset != (0, 0):
                hop(kind, offset, offset, z_next, half).wait_recv()
            forward(kind, offset, half)
        share(kind, offset)

    def serve_all(step, kind, offsets):
        @pl.when((step == 0) & (core == kind))
        def _():
            for offset in offsets:
                serve(kind, offset)

    def service(step, place):
        for kind in range(2):
            for r in range(1, ROUNDS):

                @pl.when((step == r - 1) & (core == kind))
                def _(kind=kind, r=r):
                    serve(kind, ORDER[kind][r * CHUNK + place])

    def pair_copy(kind, rows, step):
        return pltpu.make_async_remote_copy(
            src_ref=grads.at[kind, rows],
            dst_ref=sib.at[rows],
            send_sem=sib_send.at[step],
            recv_sem=sib_recv.at[step],
            device_id=sibling,
            device_id_type=MESH,
        )

    def ahead(step):
        rows = pl.ds(pl.multiple_of(step * CTOK, CTOK), CTOK)
        first = pl.multiple_of(step * 2 * CROW, 2 * CROW)
        packed = pl.ds(first, 2 * CROW)
        pick = (lax.broadcasted_iota(jnp.int32, (CAP, LANES), 1) == me).astype(F32).astype(BF16)
        row_id = lax.broadcasted_iota(jnp.int32, (CTOK, CTOK), 0)
        col_id = lax.broadcasted_iota(jnp.int32, (CTOK, CTOK), 1)
        upto = (row_id <= col_id) & (row_id // TOK == col_id // TOK)
        upto = upto.astype(F32).astype(BF16)
        base = (lax.broadcasted_iota(jnp.int32, (1, CTOK), 1) // TOK * CAP).astype(F32)
        place = lax.broadcasted_iota(jnp.int32, (CROW, CTOK), 0).astype(F32)
        weight_parts = []
        for kind in range(2):
            table = buf[kind, rows, 2 * width : 2 * width + LANES]
            weight_row = dot(pick, table, ((1,), (1,)))
            routed = jnp.where(weight_row > 0, 1.0, 0.0)
            rank = dot(routed.astype(BF16), upto)
            target = jnp.where(routed[0:1] > 0, base + rank[0:1] - 1.0, -1.0)
            select = jnp.where(place == target, 1.0, 0.0)
            weight_parts.append(jnp.sum(select * weight_row[0:1], axis=1, keepdims=True))
            back_select[kind] = select.T.astype(BF16)
            select = select.astype(BF16)
            own = pl.ds(pl.multiple_of(first + kind * CROW, CROW), CROW)
            for c in range(2 * NG):
                cols = slice((c % NG) * part, (c % NG + 1) * part)
                picked = dot(select, buf[kind, rows, c * part : (c + 1) * part])
                rows_all[c // NG, own, cols] = picked.astype(BF16)
            service(step, kind)
        weight = jnp.concatenate(weight_parts, axis=0)

        combine_grad = jnp.zeros((2 * CROW, 1), F32)
        for f in range(2):
            cols = slice(f * fhalf, (f + 1) * fhalf)
            x_rows = rows_all[0, packed, :]
            pre_gate = dot(x_rows, wg[:, cols])
            pre_up = dot(x_rows, wu[:, cols])
            back = dot(rows_all[1, packed, :], wd[cols, :], ((1,), (1,)))
            sigmoid = jax.nn.sigmoid(pre_gate)
            activation = pre_gate * sigmoid
            derivative = sigmoid * (1.0 + pre_gate * (1.0 - sigmoid))
            hidden = activation * pre_up
            combine_grad = combine_grad + jnp.sum(hidden * back, axis=1, keepdims=True)
            back = back * weight
            gate_rows = back * pre_up * derivative
            up_rows = back * activation
            pair[0, :, cols] = gate_rows.astype(BF16)
            pair[1, :, cols] = up_rows.astype(BF16)
            rows_t[0, cols, packed] = gate_rows.T.astype(BF16)
            rows_t[1, cols, packed] = up_rows.T.astype(BF16)
            rows_t[2, cols, packed] = (hidden * weight).T.astype(BF16)
            service(step, 2 + f)

        lanes = lax.broadcasted_iota(jnp.int32, (2 * CROW, LANES), 1)
        spread[...] = jnp.where(lanes == me, combine_grad, 0.0).astype(BF16)

    def behind(step, serving):
        first = pl.multiple_of(step * CTOK, CTOK)
        rows = pl.ds(first, CTOK)
        for c in range(NG):
            cols = slice(c * part, (c + 1) * part)
            row_grad = dot(pair[0], wg[cols, :], ((1,), (1,)))
            row_grad = row_grad + dot(pair[1], wu[cols, :], ((1,), (1,)))
            row_grad = row_grad.astype(BF16)
            for kind in range(2):
                mine = row_grad[kind * CROW : (kind + 1) * CROW]
                grads[kind, rows, cols] = dot(back_select[kind], mine).astype(BF16)
            if serving:
                service(step, 4 + c)
        for kind in range(2):
            mine = spread[kind * CROW : (kind + 1) * CROW, :]
            grads[kind, rows, width:grad_width] = dot(back_select[kind], mine).astype(BF16)
        pair_copy(1 - core, rows, step).start()

    def pair_sum(step):
        first = pl.multiple_of(step * CTOK, CTOK)
        pair_copy(core, pl.ds(first, CTOK), step).wait_recv()

        def piece(j, carry):
            rows = pl.ds(pl.multiple_of(first + j * TOK, TOK), TOK)
            total = grads[core, rows, :].astype(F32) + sib[rows, :].astype(F32)
            grads[core, rows, :] = total.astype(BF16)
            return carry

        lax.fori_loop(0, CHUNK, piece, 0)

    def round_body(step, carry):
        for kind in range(2):
            serve_all(step, kind, ORDER[kind][:CHUNK])

        def wait_block(i, inner):
            slot = step * CHUNK + i
            rows = pl.ds(pl.multiple_of(slot * TOK, TOK), TOK)
            pltpu.make_async_remote_copy(
                src_ref=buf.at[1 - core, rows],
                dst_ref=buf.at[1 - core, rows],
                send_sem=core_send.at[slot],
                recv_sem=ag_recv.at[((1 - core) * BLOCKS + slot) * 2],
                device_id=sibling,
                device_id_type=MESH,
            ).wait_recv()
            return inner

        lax.fori_loop(0, CHUNK, wait_block, 0)

        @pl.when(step == 0)
        def _():
            for load in loads[2:]:
                load.wait()

        ahead(step)

        @pl.when(step < ROUNDS - 1)
        def _():
            behind(step, True)

        @pl.when((step > 0) & (step < ROUNDS - 1))
        def _():
            pair_sum(step - 1)

        return carry

    lax.fori_loop(0, ROUNDS, round_body, 0)

    def tile(index, mat, half):
        left = rows_t[mat, half * fhalf : (half + 1) * fhalf, :]
        cols = pl.ds(pl.multiple_of(index * part, part), part)
        return dot(left, rows_all[0 if mat < 2 else 1, :, cols])

    def y_copy(source, step, way, mat):
        index = (step * 2 + way) * 3 + mat
        return pltpu.make_async_remote_copy(
            src_ref=source,
            dst_ref=yrecv.at[index],
            send_sem=y_send.at[index],
            recv_sem=y_recv.at[index],
            device_id=y_next if way == 0 else y_prev,
            device_id_type=MESH,
        )

    y_sent = []

    def y_task(step, mat):
        for way in range(2):
            shift = NG - 1 - step if way == 0 else 1 + step
            term = tile((group + shift) % NG, mat, way)
            if step == 0:
                source = ysend.at[way * 3 + mat]
                source[...] = term.astype(BF16)
            else:
                source = yrecv.at[((step - 1) * 2 + way) * 3 + mat]
                y_copy(source, step - 1, way, mat).wait_recv()
                term = term + source[...].astype(F32)
                if step < NG - 1:
                    source[...] = term.astype(BF16)
            if step < NG - 1:
                copy = y_copy(source, step, way, mat)
                copy.start()
                y_sent.append(copy)
            else:
                cols = slice(way * fhalf, (way + 1) * fhalf)
                if mat == 0:
                    o_gate[:, cols] = term.T.astype(BF16)
                elif mat == 1:
                    o_up[:, cols] = term.T.astype(BF16)
                else:
                    o_down[cols, :] = term.astype(BF16)

    def rows_of(ox, oz):
        a, b = slot_of(0, ox, oz), slot_of(1, ox, oz)
        return pl.multiple_of((a + (b - a) * core) * TOK, TOK)

    def block(ox, oz, half=None):
        first = rows_of(ox, oz)
        if half is None:
            return grads.at[core, pl.ds(first, TOK)]
        return grads.at[core, pl.ds(pl.multiple_of(first + half * HALF, HALF), HALF)]

    def push(source, target, send_sem, recv_sem, other):
        return pltpu.make_async_remote_copy(
            src_ref=source,
            dst_ref=target,
            send_sem=send_sem,
            recv_sem=recv_sem,
            device_id=other,
            device_id_type=MESH,
        )

    def far_copy(zi):
        return push(block(2, ZO[zi]), xfar.at[zi], xf_send.at[zi], xf_recv.at[zi], x_prev)

    def near_copy(zi):
        return push(block(-1, ZO[zi]), xnear.at[zi], xn_send.at[zi], xn_recv.at[zi], x_next)

    def last_copy():
        return push(block(1, 0), xnear.at[NZ], xn_send.at[NZ], xn_recv.at[NZ], x_prev)

    def z_copy(ox, side, k):
        index = (ox * 2 + side) * 4 + k - 1
        if k == 4:
            source = block(ox, 4, side)
            target = znear.at[index, pl.ds(side * HALF, HALF)]
        else:
            source = block(ox, (1 - 2 * side) * k)
            target = znear.at[index]
        return push(
            source, target, z_send.at[index], z_recv.at[index], z_prev if side == 0 else z_next
        )

    rs_sent = []

    def go(copy):
        copy.start()
        rs_sent.append(copy)

    def x_start():
        for zi in (7, 5, 6, 3, 4, 1, 2, 0):
            go(far_copy(zi))
            go(near_copy(zi))

    def x_total(ox, oz):
        zi = ZO.index(oz)
        came = (near_copy(zi), xnear) if ox == 0 else (far_copy(zi), xfar)
        came[0].wait_recv()
        return block(ox, oz)[...].astype(F32) + came[1][zi].astype(F32)

    def z_task(ox, oz):
        total = x_total(ox, oz)
        mine = block(ox, oz)
        if oz == 4:
            mine[...] = total.astype(BF16)
            go(z_copy(ox, 0, 4))
            go(z_copy(ox, 1, 4))
            return
        side = 0 if oz > 0 else 1
        k = abs(oz)
        index = (ox * 2 + side) * 4 + k
        z_copy(ox, side, k + 1).wait_recv()
        if k == 3:
            mine[...] = total.astype(BF16)
            mine = block(ox, oz, side)
            got = znear[index, side * HALF : (side + 1) * HALF, :]
            mine[...] = (mine[...].astype(F32) + got.astype(F32)).astype(BF16)
        else:
            mine[...] = (total + znear[index].astype(F32)).astype(BF16)
        go(z_copy(ox, side, k))

    def z_tasks(*offsets):
        for oz in offsets:
            for ox in (1, 0):
                z_task(ox, oz)

    def z_total(ox):
        total = x_total(ox, 0)
        for side in range(2):
            z_copy(ox, side, 1).wait_recv()
            total = total + znear[(ox * 2 + side) * 4].astype(F32)
        return total

    def x_last():
        block(1, 0)[...] = z_total(1).astype(BF16)
        go(last_copy())

    def z_final():
        total = z_total(0)
        last_copy().wait_recv()
        total = total + xnear[NZ].astype(F32)
        o_tokens[...] = total[:, :width].astype(BF16)
        by_expert = total[:, width:grad_width].astype(BF16)
        by_expert = dot(identity(LANES), by_expert, ((1,), (1,)))
        for k in range(top):
            named = expert_ids[k : k + 1, :] == expert_iota
            value = jnp.sum(jnp.where(named, by_expert, 0.0), axis=0, keepdims=True)
            o_combine[k : k + 1, :] = value.astype(BF16)

    for mat in range(3):
        y_task(0, mat)
    behind(ROUNDS - 1, False)
    pair_sum(ROUNDS - 2)
    pair_sum(ROUNDS - 1)
    x_start()
    y_task(1, 0)
    z_tasks(4)
    y_task(1, 1)
    z_tasks(3, -3)
    y_task(1, 2)
    z_tasks(2, -2)
    y_task(2, 0)
    z_tasks(1, -1)
    y_task(2, 1)
    x_last()
    y_task(2, 2)
    z_final()
    y_task(3, 0)
    y_task(3, 1)
    y_task(3, 2)

    for kind in range(2):

        @pl.when(core == kind)
        def _(kind=kind):
            for (target, half), (source, other) in hops[kind].items():
                hop(kind, source, target, other, half).wait_send()
            for offset in shares[kind]:
                across(kind, slot_of(kind, *offset)).wait_send()

    def pair_done(i, carry):
        pair_copy(1 - core, pl.ds(pl.multiple_of(i * CTOK, CTOK), CTOK), i).wait_send()
        return carry

    lax.fori_loop(0, BLOCKS // CHUNK, pair_done, 0)
    for copy in y_sent + rs_sent:
        copy.wait_send()


def hand_out(*refs):
    sources, targets, held, sems = refs[:5], refs[5:10], refs[10:15], refs[15]
    taken = [pltpu.make_async_copy(sources[i], held[i], sems.at[i]) for i in range(5)]
    given = [pltpu.make_async_copy(held[i], targets[i], sems.at[5 + i]) for i in range(5)]
    for copy in taken:
        copy.start()
    for before, after in zip(taken, given):
        before.wait()
        after.start()
    for copy in given:
        copy.wait()


def shards(tokens, grad_out, combine, expert_ids, w_gate, w_up, w_down):
    tok, width = tokens.shape
    top = expert_ids.shape[1]
    ff = w_gate.shape[2]
    part = width // NG
    slots = BLOCKS * TOK
    picked = 2 * ROUNDS * CROW
    gw = width + LANES
    any_spec = pl.BlockSpec(memory_space=pl.ANY)
    vmem_spec = pl.BlockSpec(memory_space=pltpu.VMEM)
    dma = pltpu.SemaphoreType.DMA
    results = pl.pallas_call(
        kernel,
        out_shape=(
            jax.ShapeDtypeStruct((tok, width), BF16),
            jax.ShapeDtypeStruct((top, tok), BF16),
            jax.ShapeDtypeStruct((part, ff), BF16),
            jax.ShapeDtypeStruct((part, ff), BF16),
            jax.ShapeDtypeStruct((ff, part), BF16),
        ),
        in_specs=[any_spec, any_spec, vmem_spec, vmem_spec, any_spec, any_spec, any_spec],
        out_specs=[vmem_spec] * 5,
        scratch_shapes=[
            pltpu.VMEM((2, slots, 2 * width + LANES), BF16),
            pltpu.VMEM((width, ff), BF16),
            pltpu.VMEM((width, ff), BF16),
            pltpu.VMEM((ff, width), BF16),
            pltpu.VMEM((2, picked, width), BF16),
            pltpu.VMEM((3, ff, picked), BF16),
            pltpu.VMEM((2, 2 * CROW, ff), BF16),
            pltpu.VMEM((2, CTOK, CROW), BF16),
            pltpu.VMEM((2 * CROW, LANES), BF16),
            pltpu.VMEM((2, slots, gw), BF16),
            pltpu.VMEM((slots, gw), BF16),
            pltpu.VMEM((6, ff // 2, part), BF16),
            pltpu.VMEM((18, ff // 2, part), BF16),
            pltpu.VMEM((NZ, tok, gw), BF16),
            pltpu.VMEM((NZ + 1, tok, gw), BF16),
            pltpu.VMEM((16, tok, gw), BF16),
            dma((5,)),
            dma((4 * BLOCKS,)),
            dma((4 * BLOCKS,)),
            dma((BLOCKS,)),
            dma((BLOCKS // CHUNK,)),
            dma((BLOCKS // CHUNK,)),
            dma((18,)),
            dma((18,)),
            dma((NZ,)),
            dma((NZ,)),
            dma((NZ + 1,)),
            dma((NZ + 1,)),
            dma((16,)),
            dma((16,)),
        ],
        compiler_params=pltpu.CompilerParams(
            collective_id=0, has_side_effects=True, vmem_limit_bytes=63 << 20
        ),
    )(tokens, grad_out, combine.T, expert_ids.T, w_gate[0], w_up[0], w_down[0])
    results = pl.pallas_call(
        hand_out,
        out_shape=tuple(jax.ShapeDtypeStruct(r.shape, r.dtype) for r in results),
        in_specs=[any_spec] * 5,
        out_specs=[any_spec] * 5,
        scratch_shapes=[pltpu.VMEM(r.shape, r.dtype) for r in results] + [dma((10,))],
    )(*results)
    g_tokens, g_combine, g_gate, g_up, g_down = results
    return g_tokens, g_combine.T, g_gate[None], g_up[None], g_down[None]


def solution(mesh):
    rows = P(("grp", "ep"), None)
    expert = P("ep", None, None)
    return jax.shard_map(
        shards,
        mesh=mesh,
        in_specs=(rows, rows, rows, rows, expert, expert, expert),
        out_specs=(rows, rows, P("ep", "grp", None), P("ep", "grp", None), P("ep", None, "grp")),
        check_vma=False,
    )
```

```python
import functools

import jax
import jax.numpy as jnp
from jax import lax
from jax.experimental import pallas as pl
from jax.experimental.pallas import tpu as pltpu
from jax.sharding import PartitionSpec as P

MESH = pl.DeviceIdType.MESH
F32 = jnp.float32
BF16 = jnp.bfloat16

NX, NZ, NG = 4, 8, 4
TOK = 32
HALF = TOK // 2
CAP = 16
LANES = 128
XO = (0, 1, -1, 2)
ZO = (0, 1, -1, 2, -2, 3, -3, 4)
BLOCKS = NX * NZ
CHUNK = 8
CTOK = CHUNK * TOK
CROW = CHUNK * CAP
ROUNDS = BLOCKS // CHUNK


ORDER = (
    (
        *((0, 0), (1, 0), (0, 1), (1, -1), (0, -1), (0, 2), (-1, -1), (1, 1)),
        *((0, -2), (-1, -2), (0, 3), (1, 2), (0, -3), (2, 0), (-1, 1), (2, -1)),
        *((2, 1), (-1, -3), (-1, 0), (0, 4), (1, -2), (-1, 2), (1, 3), (2, 2)),
        *((2, -3), (-1, 3), (-1, 4), (1, 4), (2, 3), (2, -2), (1, -3), (2, 4)),
    ),
    (
        *((0, 0), (0, 1), (0, -1), (-1, 0), (0, 2), (-1, 1), (0, -2), (1, -1)),
        *((1, 1), (0, -3), (0, 3), (2, -1), (1, 0), (1, 2), (1, -2), (-1, -2)),
        *((-1, 2), (2, 1), (0, 4), (1, 3), (2, -2), (-1, 3), (-1, -1), (-1, -3)),
        *((1, -3), (2, 0), (2, 2), (-1, 4), (2, 3), (2, -3), (1, 4), (2, 4)),
    ),
)
WAYS = (
    (
        (-1, 0, 2, 3, 3, 2, 1, 2, 3, 3, 2, 2, 3, 0, 1, 1, 0, 3, 1, 2, 3, 2, 2, 0, 1, 1, 3, 2, 0, 2, 3, 0),
        (-1, 0, 2, 3, 3, 2, 1, 0, 3, 3, 2, 2, 3, 0, 1, 1, 0, 3, 1, 3, 0, 2, 0, 0, 1, 2, 3, 2, 0, 2, 1, 3),
    ),
    (
        (-1, 2, 3, 1, 2, 1, 3, 0, 0, 3, 2, 0, 2, 2, 0, 1, 1, 0, 2, 2, 1, 1, 0, 1, 3, 3, 2, 1, 0, 1, 3, 2),
        (-1, 2, 3, 1, 2, 1, 3, 0, 0, 3, 2, 0, 0, 0, 0, 1, 1, 1, 3, 0, 1, 2, 0, 1, 3, 3, 1, 1, 0, 0, 3, 1),
    ),
)
MOVES = ((1, 0), (-1, 0), (0, 1), (0, -1))


def slot_of(kind, ox, oz):
    return ORDER[kind].index((ox, oz))


def children(kind, ox, oz, half):
    found = []
    for target, way in zip(ORDER[kind], WAYS[kind][half]):
        dx, dz = MOVES[way]
        if way >= 0 and (target[0] - ox - dx) % NX == 0 and (target[1] - oz - dz) % NZ == 0:
            found.append((target, way))
    return found


def dot(left, right, dims=((1,), (0,))):
    return lax.dot_general(left, right, (dims, ((), ())), preferred_element_type=F32)


def identity(size):
    row = lax.broadcasted_iota(jnp.int32, (size, size), 0)
    col = lax.broadcasted_iota(jnp.int32, (size, size), 1)
    return (row == col).astype(F32).astype(BF16)


def kernel(
    tokens,
    grad_out,
    combine_in,
    ids_in,
    w_gate,
    w_up,
    w_down,
    r_tokens,
    r_combine,
    r_gate,
    r_up,
    r_down,
    o_tokens,
    o_combine,
    o_gate,
    o_up,
    o_down,
    combine,
    expert_ids,
    buf,
    wg,
    wu,
    wd,
    rows_all,
    rows_t,
    pair,
    back_select,
    spread,
    grads,
    sib,
    ysend,
    yrecv,
    xfar,
    xnear,
    znear,
    in_sem,
    out_sem,
    ag_send,
    ag_recv,
    core_send,
    sib_send,
    sib_recv,
    y_send,
    y_recv,
    xf_send,
    xf_recv,
    xn_send,
    xn_recv,
    z_send,
    z_recv,
):
    width = tokens.shape[1]
    hidden_width = w_gate.shape[1]
    part = width // NG
    fhalf = hidden_width // 2
    grad_width = width + LANES
    me = lax.axis_index("ep")
    group = lax.axis_index("grp")
    core = me % 2
    zpos = (me // 2) % NZ
    xpos = me // (2 * NZ)

    def at(dx, dz):
        return {"ep": (((xpos + dx + NX) % NX) * NZ + (zpos + dz + NZ) % NZ) * 2 + core}

    sibling = {"ep": me + 1 - 2 * core}
    y_next = {"grp": (group + 1) % NG}
    y_prev = {"grp": (group + NG - 1) % NG}
    x_next, x_prev, z_next, z_prev = at(1, 0), at(-1, 0), at(0, 1), at(0, -1)

    loads = [
        pltpu.make_async_copy(tokens, buf.at[core, pl.ds(0, TOK), pl.ds(0, width)], in_sem.at[0]),
        pltpu.make_async_copy(
            grad_out, buf.at[core, pl.ds(0, TOK), pl.ds(width, width)], in_sem.at[1]
        ),
        pltpu.make_async_copy(w_gate, wg, in_sem.at[2]),
        pltpu.make_async_copy(w_up, wu, in_sem.at[3]),
        pltpu.make_async_copy(w_down, wd, in_sem.at[4]),
    ]
    narrow = [
        pltpu.make_async_copy(combine_in, combine, in_sem.at[5]),
        pltpu.make_async_copy(ids_in, expert_ids, in_sem.at[6]),
    ]
    for load in narrow + loads:
        load.start()
    barrier = pltpu.get_barrier_semaphore()
    for other in (sibling, x_next, x_prev, z_next, z_prev, y_next, y_prev):
        pl.semaphore_signal(barrier, inc=1, device_id=other, device_id_type=MESH)
    for load in narrow:
        load.wait()
    top = expert_ids.shape[0]
    expert_iota = lax.broadcasted_iota(jnp.int32, (LANES, TOK), 0)
    weights = combine[...].astype(F32)
    table = jnp.zeros((LANES, TOK), F32)
    for k in range(top):
        named = expert_ids[k : k + 1, :] == expert_iota
        table = table + jnp.where(named, weights[k : k + 1, :], 0.0)
    table = dot(identity(TOK), table.astype(BF16), ((1,), (1,)))
    buf[core, 0:TOK, 2 * width : 2 * width + LANES] = table.astype(BF16)
    loads[0].wait()
    loads[1].wait()
    pl.semaphore_wait(barrier, 7)

    hops, shares = ({}, {}), ({}, {})

    def span(slot, half):
        if half is None:
            return pl.ds(slot * TOK, TOK)
        return pl.ds(slot * TOK + half * HALF, HALF)

    def hop(kind, source, target, other, half):
        a, b = slot_of(kind, *source), slot_of(kind, *target)
        index = (kind * BLOCKS + b) * 2 + half
        return pltpu.make_async_remote_copy(
            src_ref=buf.at[kind, span(a, half)],
            dst_ref=buf.at[kind, span(b, half)],
            send_sem=ag_send.at[index],
            recv_sem=ag_recv.at[index],
            device_id=other,
            device_id_type=MESH,
        )

    def across(kind, slot):
        return pltpu.make_async_remote_copy(
            src_ref=buf.at[kind, span(slot, None)],
            dst_ref=buf.at[kind, span(slot, None)],
            send_sem=core_send.at[slot],
            recv_sem=ag_recv.at[(kind * BLOCKS + slot) * 2],
            device_id=sibling,
            device_id_type=MESH,
        )

    def forward(kind, offset, half):
        for target, way in children(kind, *offset, half):
            other = (x_next, x_prev, z_next, z_prev)[way]
            hop(kind, offset, target, other, half).start()
            hops[kind][target, half] = offset, other

    def share(kind, offset):
        across(kind, slot_of(kind, *offset)).start()
        shares[kind][offset] = True

    def serve(kind, offset):
        for half in range(2):
            if offset != (0, 0):
                hop(kind, offset, offset, z_next, half).wait_recv()
            forward(kind, offset, half)
        share(kind, offset)

    def serve_all(step, kind, offsets):
        @pl.when((step == 0) & (core == kind))
        def _():
            for offset in offsets:
                serve(kind, offset)

    def service(step, place):
        for kind in range(2):
            for r in range(1, ROUNDS):

                @pl.when((step == r - 1) & (core == kind))
                def _(kind=kind, r=r):
                    serve(kind, ORDER[kind][r * CHUNK + place])

    def pair_copy(kind, rows, step):
        return pltpu.make_async_remote_copy(
            src_ref=grads.at[kind, rows],
            dst_ref=sib.at[rows],
            send_sem=sib_send.at[step],
            recv_sem=sib_recv.at[step],
            device_id=sibling,
            device_id_type=MESH,
        )

    def wait_block(step, i, inner):
        slot = step * CHUNK + i
        rows = pl.ds(pl.multiple_of(slot * TOK, TOK), TOK)
        pltpu.make_async_remote_copy(
            src_ref=buf.at[1 - core, rows],
            dst_ref=buf.at[1 - core, rows],
            send_sem=core_send.at[slot],
            recv_sem=ag_recv.at[((1 - core) * BLOCKS + slot) * 2],
            device_id=sibling,
            device_id_type=MESH,
        ).wait_recv()
        return inner

    def ahead(step):
        rows = pl.ds(pl.multiple_of(step * CTOK, CTOK), CTOK)
        first = pl.multiple_of(step * 2 * CROW, 2 * CROW)
        packed = pl.ds(first, 2 * CROW)
        pick = (lax.broadcasted_iota(jnp.int32, (CAP, LANES), 1) == me).astype(F32).astype(BF16)
        row_id = lax.broadcasted_iota(jnp.int32, (CTOK, CTOK), 0)
        col_id = lax.broadcasted_iota(jnp.int32, (CTOK, CTOK), 1)
        upto = (row_id <= col_id) & (row_id // TOK == col_id // TOK)
        upto = upto.astype(F32).astype(BF16)
        base = (lax.broadcasted_iota(jnp.int32, (1, CTOK), 1) // TOK * CAP).astype(F32)
        place = lax.broadcasted_iota(jnp.int32, (CROW, CTOK), 0).astype(F32)
        weight_parts = []
        for turn in range(2):
            kind = core if turn == 0 else 1 - core
            if turn == 1:
                lax.fori_loop(0, CHUNK, functools.partial(wait_block, step), 0)
            table = buf[kind, rows, 2 * width : 2 * width + LANES]
            weight_row = dot(pick, table, ((1,), (1,)))
            routed = jnp.where(weight_row > 0, 1.0, 0.0)
            rank = dot(routed.astype(BF16), upto)
            target = jnp.where(routed[0:1] > 0, base + rank[0:1] - 1.0, -1.0)
            select = jnp.where(place == target, 1.0, 0.0)
            weight_parts.append(jnp.sum(select * weight_row[0:1], axis=1, keepdims=True))
            back_select[turn] = select.T.astype(BF16)
            select = select.astype(BF16)
            own = pl.ds(pl.multiple_of(first + turn * CROW, CROW), CROW)
            for c in range(2 * NG):
                cols = slice((c % NG) * part, (c % NG + 1) * part)
                picked = dot(select, buf[kind, rows, c * part : (c + 1) * part])
                rows_all[c // NG, own, cols] = picked.astype(BF16)
            service(step, turn)
        weight = jnp.concatenate(weight_parts, axis=0)

        combine_grad = jnp.zeros((2 * CROW, 1), F32)
        for f in range(2):
            cols = slice(f * fhalf, (f + 1) * fhalf)
            x_rows = rows_all[0, packed, :]
            pre_gate = dot(x_rows, wg[:, cols])
            pre_up = dot(x_rows, wu[:, cols])
            back = dot(rows_all[1, packed, :], wd[cols, :], ((1,), (1,)))
            sigmoid = jax.nn.sigmoid(pre_gate)
            activation = pre_gate * sigmoid
            derivative = sigmoid * (1.0 + pre_gate * (1.0 - sigmoid))
            hidden = activation * pre_up
            combine_grad = combine_grad + jnp.sum(hidden * back, axis=1, keepdims=True)
            back = back * weight
            gate_rows = back * pre_up * derivative
            up_rows = back * activation
            pair[0, :, cols] = gate_rows.astype(BF16)
            pair[1, :, cols] = up_rows.astype(BF16)
            rows_t[0, cols, packed] = gate_rows.T.astype(BF16)
            rows_t[1, cols, packed] = up_rows.T.astype(BF16)
            rows_t[2, cols, packed] = (hidden * weight).T.astype(BF16)
            service(step, 2 + f)

        lanes = lax.broadcasted_iota(jnp.int32, (2 * CROW, LANES), 1)
        spread[...] = jnp.where(lanes == me, combine_grad, 0.0).astype(BF16)

    def behind(step, serving):
        first = pl.multiple_of(step * CTOK, CTOK)
        rows = pl.ds(first, CTOK)
        for c in range(NG):
            cols = slice(c * part, (c + 1) * part)
            row_grad = dot(pair[0], wg[cols, :], ((1,), (1,)))
            row_grad = row_grad + dot(pair[1], wu[cols, :], ((1,), (1,)))
            row_grad = row_grad.astype(BF16)
            for turn in range(2):
                kind = core if turn == 0 else 1 - core
                mine = row_grad[turn * CROW : (turn + 1) * CROW]
                grads[kind, rows, cols] = dot(back_select[turn], mine).astype(BF16)
            if serving:
                service(step, 4 + c)
        for turn in range(2):
            kind = core if turn == 0 else 1 - core
            mine = spread[turn * CROW : (turn + 1) * CROW, :]
            grads[kind, rows, width:grad_width] = dot(back_select[turn], mine).astype(BF16)
        pair_copy(1 - core, rows, step).start()

    def pair_sum(step):
        first = pl.multiple_of(step * CTOK, CTOK)
        pair_copy(core, pl.ds(first, CTOK), step).wait_recv()

        def piece(j, carry):
            rows = pl.ds(pl.multiple_of(first + j * TOK, TOK), TOK)
            total = grads[core, rows, :].astype(F32) + sib[rows, :].astype(F32)
            grads[core, rows, :] = total.astype(BF16)
            return carry

        lax.fori_loop(0, CHUNK, piece, 0)

    def round_body(step, carry):
        for kind in range(2):
            serve_all(step, kind, ORDER[kind][:CHUNK])

        @pl.when(step == 0)
        def _():
            for load in loads[2:]:
                load.wait()

        ahead(step)

        @pl.when(step < ROUNDS - 1)
        def _():
            behind(step, True)

        @pl.when((step > 0) & (step < ROUNDS - 1))
        def _():
            pair_sum(step - 1)

        return carry

    lax.fori_loop(0, ROUNDS, round_body, 0)

    def tile(index, mat, half):
        left = rows_t[mat, half * fhalf : (half + 1) * fhalf, :]
        cols = pl.ds(pl.multiple_of(index * part, part), part)
        return dot(left, rows_all[0 if mat < 2 else 1, :, cols])

    def y_copy(source, step, way, mat):
        index = (step * 2 + way) * 3 + mat
        return pltpu.make_async_remote_copy(
            src_ref=source,
            dst_ref=yrecv.at[index],
            send_sem=y_send.at[index],
            recv_sem=y_recv.at[index],
            device_id=y_next if way == 0 else y_prev,
            device_id_type=MESH,
        )

    y_sent = []
    results = [
        pltpu.make_async_copy(o_tokens, r_tokens, out_sem.at[0]),
        pltpu.make_async_copy(o_combine, r_combine, out_sem.at[1]),
        pltpu.make_async_copy(o_gate, r_gate, out_sem.at[2]),
        pltpu.make_async_copy(o_up, r_up, out_sem.at[3]),
        pltpu.make_async_copy(o_down, r_down, out_sem.at[4]),
    ]

    def y_task(step, mat):
        for way in range(2):
            shift = NG - 1 - step if way == 0 else 1 + step
            term = tile((group + shift) % NG, mat, way)
            if step == 0:
                source = ysend.at[way * 3 + mat]
                source[...] = term.astype(BF16)
            else:
                source = yrecv.at[((step - 1) * 2 + way) * 3 + mat]
                y_copy(source, step - 1, way, mat).wait_recv()
                term = term + source[...].astype(F32)
                if step < NG - 1:
                    source[...] = term.astype(BF16)
            if step < NG - 1:
                copy = y_copy(source, step, way, mat)
                copy.start()
                y_sent.append(copy)
            else:
                cols = slice(way * fhalf, (way + 1) * fhalf)
                if mat == 0:
                    o_gate[:, cols] = term.T.astype(BF16)
                elif mat == 1:
                    o_up[:, cols] = term.T.astype(BF16)
                else:
                    o_down[cols, :] = term.astype(BF16)
        if step == NG - 1:
            results[2 + mat].start()

    def rows_of(ox, oz):
        a, b = slot_of(0, ox, oz), slot_of(1, ox, oz)
        return pl.multiple_of((a + (b - a) * core) * TOK, TOK)

    def block(ox, oz, half=None):
        first = rows_of(ox, oz)
        if half is None:
            return grads.at[core, pl.ds(first, TOK)]
        return grads.at[core, pl.ds(pl.multiple_of(first + half * HALF, HALF), HALF)]

    def push(source, target, send_sem, recv_sem, other):
        return pltpu.make_async_remote_copy(
            src_ref=source,
            dst_ref=target,
            send_sem=send_sem,
            recv_sem=recv_sem,
            device_id=other,
            device_id_type=MESH,
        )

    def far_copy(zi):
        return push(block(2, ZO[zi]), xfar.at[zi], xf_send.at[zi], xf_recv.at[zi], x_prev)

    def near_copy(zi):
        return push(block(-1, ZO[zi]), xnear.at[zi], xn_send.at[zi], xn_recv.at[zi], x_next)

    def last_copy():
        return push(block(1, 0), xnear.at[NZ], xn_send.at[NZ], xn_recv.at[NZ], x_prev)

    def z_copy(ox, side, k):
        index = (ox * 2 + side) * 4 + k - 1
        if k == 4:
            source = block(ox, 4, side)
            target = znear.at[index, pl.ds(side * HALF, HALF)]
        else:
            source = block(ox, (1 - 2 * side) * k)
            target = znear.at[index]
        return push(
            source, target, z_send.at[index], z_recv.at[index], z_prev if side == 0 else z_next
        )

    rs_sent = []

    def go(copy):
        copy.start()
        rs_sent.append(copy)

    def x_start():
        for zi in (7, 5, 6, 3, 4, 1, 2, 0):
            go(far_copy(zi))
            go(near_copy(zi))

    def x_total(ox, oz):
        zi = ZO.index(oz)
        came = (near_copy(zi), xnear) if ox == 0 else (far_copy(zi), xfar)
        came[0].wait_recv()
        return block(ox, oz)[...].astype(F32) + came[1][zi].astype(F32)

    def z_task(ox, oz):
        total = x_total(ox, oz)
        mine = block(ox, oz)
        if oz == 4:
            mine[...] = total.astype(BF16)
            go(z_copy(ox, 0, 4))
            go(z_copy(ox, 1, 4))
            return
        side = 0 if oz > 0 else 1
        k = abs(oz)
        index = (ox * 2 + side) * 4 + k
        z_copy(ox, side, k + 1).wait_recv()
        if k == 3:
            mine[...] = total.astype(BF16)
            mine = block(ox, oz, side)
            got = znear[index, side * HALF : (side + 1) * HALF, :]
            mine[...] = (mine[...].astype(F32) + got.astype(F32)).astype(BF16)
        else:
            mine[...] = (total + znear[index].astype(F32)).astype(BF16)
        go(z_copy(ox, side, k))

    def z_tasks(*offsets):
        for oz in offsets:
            for ox in (1, 0):
                z_task(ox, oz)

    def z_total(ox):
        total = x_total(ox, 0)
        for side in range(2):
            z_copy(ox, side, 1).wait_recv()
            total = total + znear[(ox * 2 + side) * 4].astype(F32)
        return total

    def x_last():
        block(1, 0)[...] = z_total(1).astype(BF16)
        go(last_copy())

    def z_final():
        total = z_total(0)
        last_copy().wait_recv()
        total = total + xnear[NZ].astype(F32)
        o_tokens[...] = total[:, :width].astype(BF16)
        by_expert = total[:, width:grad_width].astype(BF16)
        by_expert = dot(identity(LANES), by_expert, ((1,), (1,)))
        for k in range(top):
            named = expert_ids[k : k + 1, :] == expert_iota
            value = jnp.sum(jnp.where(named, by_expert, 0.0), axis=0, keepdims=True)
            o_combine[k : k + 1, :] = value.astype(BF16)
        results[0].start()
        results[1].start()

    for mat in range(3):
        y_task(0, mat)
    behind(ROUNDS - 1, False)
    pair_sum(ROUNDS - 2)
    pair_sum(ROUNDS - 1)
    x_start()
    y_task(1, 0)
    z_tasks(4)
    y_task(1, 1)
    z_tasks(3, -3)
    y_task(1, 2)
    z_tasks(2, -2)
    y_task(2, 0)
    z_tasks(1, -1)
    y_task(2, 1)
    x_last()
    y_task(2, 2)
    z_final()
    y_task(3, 0)
    y_task(3, 1)
    y_task(3, 2)

    for kind in range(2):

        @pl.when(core == kind)
        def _(kind=kind):
            for (target, half), (source, other) in hops[kind].items():
                hop(kind, source, target, other, half).wait_send()
            for offset in shares[kind]:
                across(kind, slot_of(kind, *offset)).wait_send()

    def pair_done(i, carry):
        pair_copy(1 - core, pl.ds(pl.multiple_of(i * CTOK, CTOK), CTOK), i).wait_send()
        return carry

    lax.fori_loop(0, BLOCKS // CHUNK, pair_done, 0)
    for copy in y_sent + rs_sent:
        copy.wait_send()
    for copy in results:
        copy.wait()


def hand_out(*refs):
    sources, targets, held, sems = refs[:5], refs[5:10], refs[10:15], refs[15]
    taken = [pltpu.make_async_copy(sources[i], held[i], sems.at[i]) for i in range(5)]
    given = [pltpu.make_async_copy(held[i], targets[i], sems.at[5 + i]) for i in range(5)]
    for copy in taken:
        copy.start()
    for before, after in zip(taken, given):
        before.wait()
        after.start()
    for copy in given:
        copy.wait()


def shards(tokens, grad_out, combine, expert_ids, w_gate, w_up, w_down):
    tok, width = tokens.shape
    top = expert_ids.shape[1]
    ff = w_gate.shape[2]
    part = width // NG
    slots = BLOCKS * TOK
    picked = 2 * ROUNDS * CROW
    gw = width + LANES
    any_spec = pl.BlockSpec(memory_space=pl.ANY)
    dma = pltpu.SemaphoreType.DMA
    results = pl.pallas_call(
        kernel,
        out_shape=(
            jax.ShapeDtypeStruct((tok, width), BF16),
            jax.ShapeDtypeStruct((top, tok), BF16),
            jax.ShapeDtypeStruct((part, ff), BF16),
            jax.ShapeDtypeStruct((part, ff), BF16),
            jax.ShapeDtypeStruct((ff, part), BF16),
        ),
        in_specs=[any_spec] * 7,
        out_specs=[any_spec] * 5,
        scratch_shapes=[
            pltpu.VMEM((tok, width), BF16),
            pltpu.VMEM((top, tok), BF16),
            pltpu.VMEM((part, ff), BF16),
            pltpu.VMEM((part, ff), BF16),
            pltpu.VMEM((ff, part), BF16),
            pltpu.VMEM((top, tok), BF16),
            pltpu.VMEM((top, tok), jnp.int32),
            pltpu.VMEM((2, slots, 2 * width + LANES), BF16),
            pltpu.VMEM((width, ff), BF16),
            pltpu.VMEM((width, ff), BF16),
            pltpu.VMEM((ff, width), BF16),
            pltpu.VMEM((2, picked, width), BF16),
            pltpu.VMEM((3, ff, picked), BF16),
            pltpu.VMEM((2, 2 * CROW, ff), BF16),
            pltpu.VMEM((2, CTOK, CROW), BF16),
            pltpu.VMEM((2 * CROW, LANES), BF16),
            pltpu.VMEM((2, slots, gw), BF16),
            pltpu.VMEM((slots, gw), BF16),
            pltpu.VMEM((6, ff // 2, part), BF16),
            pltpu.VMEM((18, ff // 2, part), BF16),
            pltpu.VMEM((NZ, tok, gw), BF16),
            pltpu.VMEM((NZ + 1, tok, gw), BF16),
            pltpu.VMEM((16, tok, gw), BF16),
            dma((7,)),
            dma((5,)),
            dma((4 * BLOCKS,)),
            dma((4 * BLOCKS,)),
            dma((BLOCKS,)),
            dma((BLOCKS // CHUNK,)),
            dma((BLOCKS // CHUNK,)),
            dma((18,)),
            dma((18,)),
            dma((NZ,)),
            dma((NZ,)),
            dma((NZ + 1,)),
            dma((NZ + 1,)),
            dma((16,)),
            dma((16,)),
        ],
        compiler_params=pltpu.CompilerParams(
            collective_id=0, has_side_effects=True, vmem_limit_bytes=63 << 20
        ),
    )(tokens, grad_out, combine.T, expert_ids.T, w_gate[0], w_up[0], w_down[0])
    results = pl.pallas_call(
        hand_out,
        out_shape=tuple(jax.ShapeDtypeStruct(r.shape, r.dtype) for r in results),
        in_specs=[any_spec] * 5,
        out_specs=[any_spec] * 5,
        scratch_shapes=[pltpu.VMEM(r.shape, r.dtype) for r in results] + [dma((10,))],
    )(*results)
    g_tokens, g_combine, g_gate, g_up, g_down = results
    return g_tokens, g_combine.T, g_gate[None], g_up[None], g_down[None]


def solution(mesh):
    rows = P(("grp", "ep"), None)
    expert = P("ep", None, None)
    return jax.shard_map(
        shards,
        mesh=mesh,
        in_specs=(rows, rows, rows, rows, expert, expert, expert),
        out_specs=(rows, rows, P("ep", "grp", None), P("ep", "grp", None), P("ep", None, "grp")),
        check_vma=False,
    )
```

```python
import functools

import jax
import jax.numpy as jnp
from jax import lax
from jax.experimental import pallas as pl
from jax.experimental.pallas import tpu as pltpu
from jax.sharding import PartitionSpec as P

MESH = pl.DeviceIdType.MESH
F32 = jnp.float32
BF16 = jnp.bfloat16

NX, NZ, NG = 4, 8, 4
TOK = 32
HALF = TOK // 2
CAP = 16
LANES = 128
XO = (0, 1, -1, 2)
ZO = (0, 1, -1, 2, -2, 3, -3, 4)
BLOCKS = NX * NZ
CHUNK = 8
CTOK = CHUNK * TOK
CROW = CHUNK * CAP
ROUNDS = BLOCKS // CHUNK


ORDER = (
    (
        *((0, 0), (1, 0), (0, 1), (1, -1), (0, -1), (0, 2), (-1, -1), (1, 1)),
        *((0, -2), (-1, -2), (0, 3), (1, 2), (0, -3), (2, 0), (-1, 1), (2, -1)),
        *((2, 1), (-1, -3), (-1, 0), (0, 4), (1, -2), (-1, 2), (1, 3), (2, 2)),
        *((2, -3), (-1, 3), (-1, 4), (1, 4), (2, 3), (2, -2), (1, -3), (2, 4)),
    ),
    (
        *((0, 0), (0, 1), (0, -1), (-1, 0), (0, 2), (-1, 1), (0, -2), (1, -1)),
        *((1, 1), (0, -3), (0, 3), (2, -1), (1, 0), (1, 2), (1, -2), (-1, -2)),
        *((-1, 2), (2, 1), (0, 4), (1, 3), (2, -2), (-1, 3), (-1, -1), (-1, -3)),
        *((1, -3), (2, 0), (2, 2), (-1, 4), (2, 3), (2, -3), (1, 4), (2, 4)),
    ),
)
WAYS = (
    (
        (-1, 0, 2, 3, 3, 2, 1, 2, 3, 3, 2, 2, 3, 0, 1, 1, 0, 3, 1, 2, 3, 2, 2, 0, 1, 1, 3, 2, 0, 2, 3, 0),
        (-1, 0, 2, 3, 3, 2, 1, 0, 3, 3, 2, 2, 3, 0, 1, 1, 0, 3, 1, 3, 0, 2, 0, 0, 1, 2, 3, 2, 0, 2, 1, 3),
    ),
    (
        (-1, 2, 3, 1, 2, 1, 3, 0, 0, 3, 2, 0, 2, 2, 0, 1, 1, 0, 2, 2, 1, 1, 0, 1, 3, 3, 2, 1, 0, 1, 3, 2),
        (-1, 2, 3, 1, 2, 1, 3, 0, 0, 3, 2, 0, 0, 0, 0, 1, 1, 1, 3, 0, 1, 2, 0, 1, 3, 3, 1, 1, 0, 0, 3, 1),
    ),
)
MOVES = ((1, 0), (-1, 0), (0, 1), (0, -1))


def slot_of(kind, ox, oz):
    return ORDER[kind].index((ox, oz))


def children(kind, ox, oz, half):
    found = []
    for target, way in zip(ORDER[kind], WAYS[kind][half]):
        dx, dz = MOVES[way]
        if way >= 0 and (target[0] - ox - dx) % NX == 0 and (target[1] - oz - dz) % NZ == 0:
            found.append((target, way))
    return found


def dot(left, right, dims=((1,), (0,))):
    return lax.dot_general(left, right, (dims, ((), ())), preferred_element_type=F32)


def identity(size):
    row = lax.broadcasted_iota(jnp.int32, (size, size), 0)
    col = lax.broadcasted_iota(jnp.int32, (size, size), 1)
    return (row == col).astype(F32).astype(BF16)


def kernel(
    tokens,
    grad_out,
    combine_in,
    ids_in,
    w_gate,
    w_up,
    w_down,
    r_tokens,
    r_combine,
    r_gate,
    r_up,
    r_down,
    o_tokens,
    o_combine,
    o_gate,
    o_up,
    o_down,
    combine,
    expert_ids,
    buf,
    wg,
    wu,
    wd,
    rows_all,
    rows_t,
    pair,
    back_select,
    spread,
    grads,
    sib,
    ysend,
    yrecv,
    xfar,
    xnear,
    znear,
    in_sem,
    out_sem,
    ag_send,
    ag_recv,
    core_send,
    sib_send,
    sib_recv,
    y_send,
    y_recv,
    xf_send,
    xf_recv,
    xn_send,
    xn_recv,
    z_send,
    z_recv,
):
    width = tokens.shape[1]
    hidden_width = w_gate.shape[1]
    part = width // NG
    fhalf = hidden_width // 2
    grad_width = width + LANES
    me = lax.axis_index("ep")
    group = lax.axis_index("grp")
    core = me % 2
    zpos = (me // 2) % NZ
    xpos = me // (2 * NZ)

    def at(dx, dz):
        return {"ep": (((xpos + dx + NX) % NX) * NZ + (zpos + dz + NZ) % NZ) * 2 + core}

    sibling = {"ep": me + 1 - 2 * core}
    y_next = {"grp": (group + 1) % NG}
    y_prev = {"grp": (group + NG - 1) % NG}
    x_next, x_prev, z_next, z_prev = at(1, 0), at(-1, 0), at(0, 1), at(0, -1)

    loads = [
        pltpu.make_async_copy(tokens, buf.at[core, pl.ds(0, TOK), pl.ds(0, width)], in_sem.at[0]),
        pltpu.make_async_copy(
            grad_out, buf.at[core, pl.ds(0, TOK), pl.ds(width, width)], in_sem.at[1]
        ),
        pltpu.make_async_copy(w_gate, wg, in_sem.at[2]),
        pltpu.make_async_copy(w_up, wu, in_sem.at[3]),
        pltpu.make_async_copy(w_down, wd, in_sem.at[4]),
    ]
    narrow = [
        pltpu.make_async_copy(combine_in, combine, in_sem.at[5]),
        pltpu.make_async_copy(ids_in, expert_ids, in_sem.at[6]),
    ]
    for load in narrow + loads:
        load.start()
    barrier = pltpu.get_barrier_semaphore()
    for other in (sibling, x_next, x_prev, z_next, z_prev, y_next, y_prev):
        pl.semaphore_signal(barrier, inc=1, device_id=other, device_id_type=MESH)
    for load in narrow:
        load.wait()
    top = expert_ids.shape[0]
    expert_iota = lax.broadcasted_iota(jnp.int32, (LANES, TOK), 0)
    weights = combine[...].astype(F32)
    table = jnp.zeros((LANES, TOK), F32)
    for k in range(top):
        named = expert_ids[k : k + 1, :] == expert_iota
        table = table + jnp.where(named, weights[k : k + 1, :], 0.0)
    table = dot(identity(TOK), table.astype(BF16), ((1,), (1,)))
    buf[core, 0:TOK, 2 * width : 2 * width + LANES] = table.astype(BF16)
    loads[0].wait()
    loads[1].wait()
    pl.semaphore_wait(barrier, 7)

    hops, shares = ({}, {}), ({}, {})

    def span(slot, half):
        if half is None:
            return pl.ds(slot * TOK, TOK)
        return pl.ds(slot * TOK + half * HALF, HALF)

    def hop(kind, source, target, other, half):
        a, b = slot_of(kind, *source), slot_of(kind, *target)
        index = (kind * BLOCKS + b) * 2 + half
        return pltpu.make_async_remote_copy(
            src_ref=buf.at[kind, span(a, half)],
            dst_ref=buf.at[kind, span(b, half)],
            send_sem=ag_send.at[index],
            recv_sem=ag_recv.at[index],
            device_id=other,
            device_id_type=MESH,
        )

    def across(kind, slot):
        return pltpu.make_async_remote_copy(
            src_ref=buf.at[kind, span(slot, None)],
            dst_ref=buf.at[kind, span(slot, None)],
            send_sem=core_send.at[slot],
            recv_sem=ag_recv.at[(kind * BLOCKS + slot) * 2],
            device_id=sibling,
            device_id_type=MESH,
        )

    def forward(kind, offset, half):
        for target, way in children(kind, *offset, half):
            other = (x_next, x_prev, z_next, z_prev)[way]
            hop(kind, offset, target, other, half).start()
            hops[kind][target, half] = offset, other

    def share(kind, offset):
        across(kind, slot_of(kind, *offset)).start()
        shares[kind][offset] = True

    def serve(kind, offset):
        for half in range(2):
            if offset != (0, 0):
                hop(kind, offset, offset, z_next, half).wait_recv()
            forward(kind, offset, half)
        share(kind, offset)

    def serve_all(step, kind, offsets):
        @pl.when((step == 0) & (core == kind))
        def _():
            for offset in offsets:
                serve(kind, offset)

    def service(step, place):
        for kind in range(2):
            for r in range(1, ROUNDS):

                @pl.when((step == r - 1) & (core == kind))
                def _(kind=kind, r=r):
                    serve(kind, ORDER[kind][r * CHUNK + place])

    def pair_copy(kind, rows, step):
        return pltpu.make_async_remote_copy(
            src_ref=grads.at[kind, rows],
            dst_ref=sib.at[rows],
            send_sem=sib_send.at[step],
            recv_sem=sib_recv.at[step],
            device_id=sibling,
            device_id_type=MESH,
        )

    def wait_block(step, i, inner):
        slot = step * CHUNK + i
        rows = pl.ds(pl.multiple_of(slot * TOK, TOK), TOK)
        pltpu.make_async_remote_copy(
            src_ref=buf.at[1 - core, rows],
            dst_ref=buf.at[1 - core, rows],
            send_sem=core_send.at[slot],
            recv_sem=ag_recv.at[((1 - core) * BLOCKS + slot) * 2],
            device_id=sibling,
            device_id_type=MESH,
        ).wait_recv()
        return inner

    def ahead(step):
        rows = pl.ds(pl.multiple_of(step * CTOK, CTOK), CTOK)
        first = pl.multiple_of(step * 2 * CROW, 2 * CROW)
        packed = pl.ds(first, 2 * CROW)
        pick = (lax.broadcasted_iota(jnp.int32, (CAP, LANES), 1) == me).astype(F32).astype(BF16)
        row_id = lax.broadcasted_iota(jnp.int32, (CTOK, CTOK), 0)
        col_id = lax.broadcasted_iota(jnp.int32, (CTOK, CTOK), 1)
        upto = (row_id <= col_id) & (row_id // TOK == col_id // TOK)
        upto = upto.astype(F32).astype(BF16)
        base = (lax.broadcasted_iota(jnp.int32, (1, CTOK), 1) // TOK * CAP).astype(F32)
        place = lax.broadcasted_iota(jnp.int32, (CROW, CTOK), 0).astype(F32)
        weight_parts = []
        for turn in range(2):
            kind = core if turn == 0 else 1 - core
            if turn == 1:
                lax.fori_loop(0, CHUNK, functools.partial(wait_block, step), 0)
            table = buf[kind, rows, 2 * width : 2 * width + LANES]
            weight_row = dot(pick, table, ((1,), (1,)))
            routed = jnp.where(weight_row > 0, 1.0, 0.0)
            rank = dot(routed.astype(BF16), upto)
            target = jnp.where(routed[0:1] > 0, base + rank[0:1] - 1.0, -1.0)
            select = jnp.where(place == target, 1.0, 0.0)
            weight_parts.append(jnp.sum(select * weight_row[0:1], axis=1, keepdims=True))
            back_select[turn] = select.T.astype(BF16)
            select = select.astype(BF16)
            own = pl.ds(pl.multiple_of(first + turn * CROW, CROW), CROW)
            for c in range(2 * NG):
                cols = slice((c % NG) * part, (c % NG + 1) * part)
                picked = dot(select, buf[kind, rows, c * part : (c + 1) * part])
                rows_all[c // NG, own, cols] = picked.astype(BF16)
            service(step, turn)
        weight = jnp.concatenate(weight_parts, axis=0)

        combine_grad = jnp.zeros((2 * CROW, 1), F32)
        for f in range(2):
            cols = slice(f * fhalf, (f + 1) * fhalf)
            x_rows = rows_all[0, packed, :]
            pre_gate = dot(x_rows, wg[:, cols])
            pre_up = dot(x_rows, wu[:, cols])
            back = dot(rows_all[1, packed, :], wd[cols, :], ((1,), (1,)))
            sigmoid = jax.nn.sigmoid(pre_gate)
            activation = pre_gate * sigmoid
            derivative = sigmoid * (1.0 + pre_gate * (1.0 - sigmoid))
            hidden = activation * pre_up
            combine_grad = combine_grad + jnp.sum(hidden * back, axis=1, keepdims=True)
            back = back * weight
            gate_rows = back * pre_up * derivative
            up_rows = back * activation
            pair[0, :, cols] = gate_rows.astype(BF16)
            pair[1, :, cols] = up_rows.astype(BF16)
            rows_t[0, cols, packed] = gate_rows.T.astype(BF16)
            rows_t[1, cols, packed] = up_rows.T.astype(BF16)
            rows_t[2, cols, packed] = (hidden * weight).T.astype(BF16)
            service(step, 2 + f)

        lanes = lax.broadcasted_iota(jnp.int32, (2 * CROW, LANES), 1)
        spread[...] = jnp.where(lanes == me, combine_grad, 0.0).astype(BF16)

    def behind(step, serving):
        first = pl.multiple_of(step * CTOK, CTOK)
        rows = pl.ds(first, CTOK)
        for c in range(NG):
            cols = slice(c * part, (c + 1) * part)
            row_grad = dot(pair[0], wg[cols, :], ((1,), (1,)))
            row_grad = row_grad + dot(pair[1], wu[cols, :], ((1,), (1,)))
            row_grad = row_grad.astype(BF16)
            for turn in range(2):
                kind = core if turn == 0 else 1 - core
                mine = row_grad[turn * CROW : (turn + 1) * CROW]
                grads[kind, rows, cols] = dot(back_select[turn], mine).astype(BF16)
            if serving:
                service(step, 4 + c)
        for turn in range(2):
            kind = core if turn == 0 else 1 - core
            mine = spread[turn * CROW : (turn + 1) * CROW, :]
            grads[kind, rows, width:grad_width] = dot(back_select[turn], mine).astype(BF16)
        pair_copy(1 - core, rows, step).start()

    def pair_sum(step):
        first = pl.multiple_of(step * CTOK, CTOK)
        pair_copy(core, pl.ds(first, CTOK), step).wait_recv()

        def piece(j, carry):
            rows = pl.ds(pl.multiple_of(first + j * TOK, TOK), TOK)
            total = grads[core, rows, :].astype(F32) + sib[rows, :].astype(F32)
            grads[core, rows, :] = total.astype(BF16)
            return carry

        lax.fori_loop(0, CHUNK, piece, 0)

    def round_body(step, carry):
        for kind in range(2):
            serve_all(step, kind, ORDER[kind][:CHUNK])

        @pl.when(step == 0)
        def _():
            for load in loads[2:]:
                load.wait()

        ahead(step)

        @pl.when(step < ROUNDS - 1)
        def _():
            behind(step, True)

        @pl.when((step > 0) & (step < ROUNDS - 1))
        def _():
            pair_sum(step - 1)

        return carry

    lax.fori_loop(0, ROUNDS, round_body, 0)

    def tile(index, mat, half):
        left = rows_t[mat, half * fhalf : (half + 1) * fhalf, :]
        cols = pl.ds(pl.multiple_of(index * part, part), part)
        return dot(left, rows_all[0 if mat < 2 else 1, :, cols])

    def y_copy(source, step, way, mat):
        index = (step * 2 + way) * 3 + mat
        return pltpu.make_async_remote_copy(
            src_ref=source,
            dst_ref=yrecv.at[index],
            send_sem=y_send.at[index],
            recv_sem=y_recv.at[index],
            device_id=y_next if way == 0 else y_prev,
            device_id_type=MESH,
        )

    y_sent = []
    results = [
        pltpu.make_async_copy(o_tokens, r_tokens, out_sem.at[0]),
        pltpu.make_async_copy(o_combine, r_combine, out_sem.at[1]),
        pltpu.make_async_copy(o_gate, r_gate, out_sem.at[2]),
        pltpu.make_async_copy(o_up, r_up, out_sem.at[3]),
        pltpu.make_async_copy(o_down, r_down, out_sem.at[4]),
    ]

    def y_task(step, mat):
        for way in range(2):
            if step < NG - 1:
                shift = NG - 1 - step if way == 0 else 1 + step
                term = tile((group + shift) % NG, mat, way)
            else:
                term = ysend[way * 3 + mat].astype(F32)
            if step == 0:
                source = ysend.at[way * 3 + mat]
                source[...] = term.astype(BF16)
            else:
                source = yrecv.at[((step - 1) * 2 + way) * 3 + mat]
                y_copy(source, step - 1, way, mat).wait_recv()
                term = term + source[...].astype(F32)
                if step < NG - 1:
                    source[...] = term.astype(BF16)
            if step < NG - 1:
                copy = y_copy(source, step, way, mat)
                copy.start()
                if step > 0:
                    y_sent.append(copy)
            else:
                cols = slice(way * fhalf, (way + 1) * fhalf)
                if mat == 0:
                    o_gate[:, cols] = term.T.astype(BF16)
                elif mat == 1:
                    o_up[:, cols] = term.T.astype(BF16)
                else:
                    o_down[cols, :] = term.astype(BF16)
        if step == NG - 1:
            results[2 + mat].start()

    def own_terms():
        for way in range(2):
            for mat in range(3):
                held = ysend.at[way * 3 + mat]
                y_copy(held, 0, way, mat).wait_send()
                held[...] = tile(group, mat, way).astype(BF16)

    def rows_of(ox, oz):
        a, b = slot_of(0, ox, oz), slot_of(1, ox, oz)
        return pl.multiple_of((a + (b - a) * core) * TOK, TOK)

    def block(ox, oz, half=None):
        first = rows_of(ox, oz)
        if half is None:
            return grads.at[core, pl.ds(first, TOK)]
        return grads.at[core, pl.ds(pl.multiple_of(first + half * HALF, HALF), HALF)]

    def push(source, target, send_sem, recv_sem, other):
        return pltpu.make_async_remote_copy(
            src_ref=source,
            dst_ref=target,
            send_sem=send_sem,
            recv_sem=recv_sem,
            device_id=other,
            device_id_type=MESH,
        )

    def far_copy(zi):
        return push(block(2, ZO[zi]), xfar.at[zi], xf_send.at[zi], xf_recv.at[zi], x_prev)

    def near_copy(zi):
        return push(block(-1, ZO[zi]), xnear.at[zi], xn_send.at[zi], xn_recv.at[zi], x_next)

    def last_copy():
        return push(block(1, 0), xnear.at[NZ], xn_send.at[NZ], xn_recv.at[NZ], x_prev)

    def z_copy(ox, side, k):
        index = (ox * 2 + side) * 4 + k - 1
        if k == 4:
            source = block(ox, 4, side)
            target = znear.at[index, pl.ds(side * HALF, HALF)]
        else:
            source = block(ox, (1 - 2 * side) * k)
            target = znear.at[index]
        return push(
            source, target, z_send.at[index], z_recv.at[index], z_prev if side == 0 else z_next
        )

    rs_sent = []

    def go(copy):
        copy.start()
        rs_sent.append(copy)

    def x_start():
        for zi in (7, 5, 6, 3, 4, 1, 2, 0):
            go(far_copy(zi))
            go(near_copy(zi))

    def x_total(ox, oz):
        zi = ZO.index(oz)
        came = (near_copy(zi), xnear) if ox == 0 else (far_copy(zi), xfar)
        came[0].wait_recv()
        return block(ox, oz)[...].astype(F32) + came[1][zi].astype(F32)

    def z_task(ox, oz):
        total = x_total(ox, oz)
        mine = block(ox, oz)
        if oz == 4:
            mine[...] = total.astype(BF16)
            go(z_copy(ox, 0, 4))
            go(z_copy(ox, 1, 4))
            return
        side = 0 if oz > 0 else 1
        k = abs(oz)
        index = (ox * 2 + side) * 4 + k
        z_copy(ox, side, k + 1).wait_recv()
        if k == 3:
            mine[...] = total.astype(BF16)
            mine = block(ox, oz, side)
            got = znear[index, side * HALF : (side + 1) * HALF, :]
            mine[...] = (mine[...].astype(F32) + got.astype(F32)).astype(BF16)
        else:
            mine[...] = (total + znear[index].astype(F32)).astype(BF16)
        go(z_copy(ox, side, k))

    def z_tasks(*offsets):
        for oz in offsets:
            for ox in (1, 0):
                z_task(ox, oz)

    def z_total(ox):
        total = x_total(ox, 0)
        for side in range(2):
            z_copy(ox, side, 1).wait_recv()
            total = total + znear[(ox * 2 + side) * 4].astype(F32)
        return total

    def x_last():
        block(1, 0)[...] = z_total(1).astype(BF16)
        go(last_copy())

    def z_final():
        total = z_total(0)
        last_copy().wait_recv()
        total = total + xnear[NZ].astype(F32)
        o_tokens[...] = total[:, :width].astype(BF16)
        by_expert = total[:, width:grad_width].astype(BF16)
        by_expert = dot(identity(LANES), by_expert, ((1,), (1,)))
        for k in range(top):
            named = expert_ids[k : k + 1, :] == expert_iota
            value = jnp.sum(jnp.where(named, by_expert, 0.0), axis=0, keepdims=True)
            o_combine[k : k + 1, :] = value.astype(BF16)
        results[0].start()
        results[1].start()

    for mat in range(3):
        y_task(0, mat)
    behind(ROUNDS - 1, False)
    pair_sum(ROUNDS - 2)
    pair_sum(ROUNDS - 1)
    x_start()
    y_task(1, 0)
    z_tasks(4)
    y_task(1, 1)
    z_tasks(3, -3)
    y_task(1, 2)
    z_tasks(2, -2)
    y_task(2, 0)
    z_tasks(1, -1)
    y_task(2, 1)
    x_last()
    y_task(2, 2)
    own_terms()
    z_final()
    y_task(3, 0)
    y_task(3, 1)
    y_task(3, 2)

    for kind in range(2):

        @pl.when(core == kind)
        def _(kind=kind):
            for (target, half), (source, other) in hops[kind].items():
                hop(kind, source, target, other, half).wait_send()
            for offset in shares[kind]:
                across(kind, slot_of(kind, *offset)).wait_send()

    def pair_done(i, carry):
        pair_copy(1 - core, pl.ds(pl.multiple_of(i * CTOK, CTOK), CTOK), i).wait_send()
        return carry

    lax.fori_loop(0, BLOCKS // CHUNK, pair_done, 0)
    for copy in y_sent + rs_sent:
        copy.wait_send()
    for copy in results:
        copy.wait()


def hand_out(*refs):
    sources, targets, held, sems = refs[:5], refs[5:10], refs[10:15], refs[15]
    taken = [pltpu.make_async_copy(sources[i], held[i], sems.at[i]) for i in range(5)]
    given = [pltpu.make_async_copy(held[i], targets[i], sems.at[5 + i]) for i in range(5)]
    for copy in taken:
        copy.start()
    for before, after in zip(taken, given):
        before.wait()
        after.start()
    for copy in given:
        copy.wait()


def shards(tokens, grad_out, combine, expert_ids, w_gate, w_up, w_down):
    tok, width = tokens.shape
    top = expert_ids.shape[1]
    ff = w_gate.shape[2]
    part = width // NG
    slots = BLOCKS * TOK
    picked = 2 * ROUNDS * CROW
    gw = width + LANES
    any_spec = pl.BlockSpec(memory_space=pl.ANY)
    dma = pltpu.SemaphoreType.DMA
    results = pl.pallas_call(
        kernel,
        out_shape=(
            jax.ShapeDtypeStruct((tok, width), BF16),
            jax.ShapeDtypeStruct((top, tok), BF16),
            jax.ShapeDtypeStruct((part, ff), BF16),
            jax.ShapeDtypeStruct((part, ff), BF16),
            jax.ShapeDtypeStruct((ff, part), BF16),
        ),
        in_specs=[any_spec] * 7,
        out_specs=[any_spec] * 5,
        scratch_shapes=[
            pltpu.VMEM((tok, width), BF16),
            pltpu.VMEM((top, tok), BF16),
            pltpu.VMEM((part, ff), BF16),
            pltpu.VMEM((part, ff), BF16),
            pltpu.VMEM((ff, part), BF16),
            pltpu.VMEM((top, tok), BF16),
            pltpu.VMEM((top, tok), jnp.int32),
            pltpu.VMEM((2, slots, 2 * width + LANES), BF16),
            pltpu.VMEM((width, ff), BF16),
            pltpu.VMEM((width, ff), BF16),
            pltpu.VMEM((ff, width), BF16),
            pltpu.VMEM((2, picked, width), BF16),
            pltpu.VMEM((3, ff, picked), BF16),
            pltpu.VMEM((2, 2 * CROW, ff), BF16),
            pltpu.VMEM((2, CTOK, CROW), BF16),
            pltpu.VMEM((2 * CROW, LANES), BF16),
            pltpu.VMEM((2, slots, gw), BF16),
            pltpu.VMEM((slots, gw), BF16),
            pltpu.VMEM((6, ff // 2, part), BF16),
            pltpu.VMEM((18, ff // 2, part), BF16),
            pltpu.VMEM((NZ, tok, gw), BF16),
            pltpu.VMEM((NZ + 1, tok, gw), BF16),
            pltpu.VMEM((16, tok, gw), BF16),
            dma((7,)),
            dma((5,)),
            dma((4 * BLOCKS,)),
            dma((4 * BLOCKS,)),
            dma((BLOCKS,)),
            dma((BLOCKS // CHUNK,)),
            dma((BLOCKS // CHUNK,)),
            dma((18,)),
            dma((18,)),
            dma((NZ,)),
            dma((NZ,)),
            dma((NZ + 1,)),
            dma((NZ + 1,)),
            dma((16,)),
            dma((16,)),
        ],
        compiler_params=pltpu.CompilerParams(
            collective_id=0, has_side_effects=True, vmem_limit_bytes=63 << 20
        ),
    )(tokens, grad_out, combine.T, expert_ids.T, w_gate[0], w_up[0], w_down[0])
    results = pl.pallas_call(
        hand_out,
        out_shape=tuple(jax.ShapeDtypeStruct(r.shape, r.dtype) for r in results),
        in_specs=[any_spec] * 5,
        out_specs=[any_spec] * 5,
        scratch_shapes=[pltpu.VMEM(r.shape, r.dtype) for r in results] + [dma((10,))],
    )(*results)
    g_tokens, g_combine, g_gate, g_up, g_down = results
    return g_tokens, g_combine.T, g_gate[None], g_up[None], g_down[None]


def solution(mesh):
    rows = P(("grp", "ep"), None)
    expert = P("ep", None, None)
    return jax.shard_map(
        shards,
        mesh=mesh,
        in_specs=(rows, rows, rows, rows, expert, expert, expert),
        out_specs=(rows, rows, P("ep", "grp", None), P("ep", "grp", None), P("ep", None, "grp")),
        check_vma=False,
    )
```
